512 devices in a mesh: dp: 2 (over core), expert: 16 (over x, y), tensor: 16 (over z).
Axes of the slice: x: 4, y: 4, z: 16, core: 2. Of those that a mesh axis runs over, the one named last changes fastest.
Arguments:
- out_grad: bfloat16 [4096, 4096], P(('dp', 'expert', 'tensor')), may hold values from -1.5 to 1.5
- routing: int32 [4096, 2], P(('dp', 'expert')), may hold values from 0 to 15, all different within a row; in each aligned block of 128 rows (0 to 127, 128 to 255, ...) at most 32 rows name the same one
- gate_codes: int32 [4096, 2], P(('dp', 'expert')), may hold values from 16 to 255
- hidden_saved: bfloat16 [2, 16, 16, 32, 12288], P('dp', 'expert', None, None, 'tensor'), may hold values from -6 to 6
- down_weight: bfloat16 [16, 12288, 4096], P('expert', 'tensor', 'dp'), may hold values from -0.0546875 to 0.0546875
- channel_scale: bfloat16 [16, 4096], P('expert', 'dp'), may hold values from 0.0029907227 to 0.029907227
Outputs:
- hidden_grad: bfloat16 [2, 16, 16, 32, 12288], P('dp', 'expert', None, None, 'tensor')
- scale_grad: float32 [16, 4096], P('expert', 'dp')
- gate_grad: float32 [4096, 2], P(('dp', 'expert', 'tensor'))
The draws below stay inside these ranges and needn't reach their ends.
Inputs may be any that keep to these rules, and one draw needn't show every extreme that they name: `routing`: each token names two different experts; in each aligned block of 128 tokens no expert is named by more than 32 routes; some block reaches 32.
All inputs are finite; a program needn't handle non-finite values.
Results may differ from the reference program's by a relative error of at most 0.0049.
Values may be sent and summed in bfloat16 or wider, within the bound.
A program may use at most 128 MiB of HBM per device.

```python
import math
import jax
import jax.numpy as jnp
import numpy as np
from jax import lax

D = 4096
FF = 12288
DATA = 2
EXPERTS = 16
SOURCES = 16
GROUP = 128
TOKENS = 4096
CAP = 32


def with_ends(values, own_key, low, high):
    dims = values.shape
    spot = [jax.random.randint(jax.random.fold_in(own_key, axis), (), 0, dims[axis]) for axis in range(len(dims))]
    values = values.at[tuple(spot)].set(low)
    longest = dims.index(max(dims))
    spot[longest] = (spot[longest] + 1) % dims[longest]
    return values.at[tuple(spot)].set(high)


def steps_of(key, extent, pieces, low, high):
    loudness = 1.0
    for axis_at, blocks in pieces:
        heights = jax.random.uniform(jax.random.fold_in(jax.random.fold_in(key, 6), axis_at), (blocks,), jnp.float32, low / len(pieces), high / len(pieces))
        loudness = loudness * jnp.repeat(jnp.exp(heights), extent[axis_at] // blocks).reshape((-1,) + (1,) * (len(extent) - 1 - axis_at))
    return loudness


def deal_out(own_key, own, number, rows, number_of, top, reach, lean):
    ranking = jax.random.permutation(own_key, number_of)
    heavy_load, ordinary = shares(number_of, rows * top, reach, lean, True), shares(number_of, rows * top, reach, lean, False)
    places = jnp.arange(number_of)

    def named(tallies, offset_by):
        used = int((tallies > 0).sum())
        fixed = max(1, used // 4)
        moved = fixed + (places - fixed + offset_by * (used - fixed)) % max(1, number_of - fixed)
        return jnp.zeros((number_of,), jnp.int32).at[ranking[jnp.where(places < fixed, places, moved)]].set(jnp.asarray(tallies, jnp.int32))

    tallies = jnp.where(number % 4 == 0, named(heavy_load, number // 4), named(ordinary, number - number // 4 - 1))
    mixed = jax.random.permutation(jax.random.fold_in(own, 3), number_of)
    donor, taker = mixed[0:number_of // 2 * 2:2], mixed[1:number_of // 2 * 2:2]
    room = jnp.minimum(tallies[donor] - 1, reach - tallies[taker]) // 2
    room = jnp.where((donor == ranking[0]) | (taker == ranking[0]) | (tallies[taker] == 0), 0, jnp.maximum(room, 0))
    moved = jax.random.randint(jax.random.fold_in(own, 4), (number_of // 2,), 0, 1 << 20) % (room + 1)
    tallies = tallies.at[donor].add(-moved).at[taker].add(moved)
    members = jnp.searchsorted(jnp.cumsum(tallies), jnp.arange(rows * top), side="right").astype(jnp.int32)
    listing = members.reshape(top, rows).T
    listing = listing[jax.random.permutation(jax.random.fold_in(own, 1), rows)]
    offset_by = jax.random.randint(jax.random.fold_in(own, 2), (rows, 1), 0, top)
    return jnp.take_along_axis(listing, (jnp.arange(top)[None, :] + offset_by) % top, axis=1)


def shares(amount, total, bound, lean, full):
    portions = [(1 << 20) // math.isqrt(grade ** lean) + 1 for grade in range(1, amount + 1)]
    largest = bound if full else min(bound, max(-(-total // amount), total * portions[0] // sum(portions)))
    least = 1 if total - largest >= amount - 1 else 0
    given, spare = [largest] + [least] * (amount - 1), total - largest - least * (amount - 1)
    while spare > 0:
        free = [i for i in range(1, amount) if given[i] < largest] or [i for i in range(1, amount) if given[i] < bound]
        pool, left = sum([portions[i] for i in free]), spare
        for i in free:
            addition = min(bound - given[i], max(1, left * portions[i] // pool), spare)
            given[i] = given[i] + addition
            spare = spare - addition
    return np.array(given)


def normal_values(own_key, extent, spread, most, cuts=(), kind=jnp.bfloat16):
    gain = steps_of(own_key, extent, cuts, -0.22, 0.18) if cuts else 1.0
    drawn = jax.random.normal(own_key, extent, jnp.float32) * spread * gain
    return jnp.minimum(jnp.maximum(drawn, -most), most).astype(kind)


def setup_inputs(seed: int = 0) -> dict:
    key_of = jax.random.split(jax.random.key(seed), 7)
    out_grad = normal_values(key_of[0], (TOKENS, D), 0.25, 1.5, ((0, 512),))
    routing_keys = jax.random.split(jax.random.fold_in(key_of[1], 1), TOKENS // GROUP)
    routing_turns = jax.random.permutation(jax.random.fold_in(key_of[1], 3), TOKENS // GROUP)
    routing = jax.vmap(lambda own, number: deal_out(jax.random.fold_in(key_of[1], 2), own, number, GROUP, EXPERTS, 2, CAP, 1))(routing_keys, routing_turns).reshape((TOKENS, 2))
    gate_codes = with_ends(jax.random.randint(key_of[2], (TOKENS, 2), 16, 256), jax.random.fold_in(key_of[2], 1), 16, 255).astype(jnp.int32)
    hidden_saved = normal_values(key_of[3], (DATA, EXPERTS, SOURCES, CAP, FF), 1.0, 6.0, ((0, 2), (1, 16), (4, 16)))
    down_weight = normal_values(key_of[4], (EXPERTS, FF, D), FF ** -0.5, 0.0546875, ((0, 16), (1, 16), (2, 2)))
    channel_scale = jnp.clip(jnp.exp(math.log(0.029907227) - 2.3025851 * jax.random.uniform(key_of[5], (EXPERTS, D), jnp.float32) ** steps_of(key_of[5], (EXPERTS, D), ((0, 16), (1, 2)), -0.2, 0.2)), 0.0029907227, 0.029907227).astype(jnp.bfloat16)
    return dict(out_grad=out_grad, routing=routing, gate_codes=gate_codes, hidden_saved=hidden_saved, down_weight=down_weight, channel_scale=channel_scale)


def slot_places(routing):
    groups = DATA * SOURCES
    pair_expert = routing.reshape(groups, GROUP * 2)
    onehot = (pair_expert[:, :, None] == jnp.arange(EXPERTS, dtype=jnp.int32)[None, None, :]).astype(jnp.int32)
    before = jnp.cumsum(onehot, axis=1) - onehot
    place_count = jnp.sum(before * onehot, axis=2)
    return (pair_expert * CAP + place_count).astype(jnp.int32)


def one_expert(inputs_one):
    weight, scale_row, grad_rows, gate_rows, saved_rows = inputs_one
    scale_wide = scale_row.astype(jnp.float32)[None, :]
    ratio_values = weight.astype(jnp.float32) / scale_wide
    bent_ratio = jnp.tanh(ratio_values)
    quantized = (scale_wide * bent_ratio).astype(jnp.bfloat16)
    slope_values = bent_ratio - ratio_values * (1.0 - bent_ratio * bent_ratio)
    summed = jnp.zeros((D,), jnp.float32)
    hidden_list = []
    gate_list = []
    for member in range(DATA):
        raw_grad = lax.dot_general(grad_rows[member], quantized, (((1,), (1,)), ((), ())), preferred_element_type=jnp.float32)
        hidden_list.append((gate_rows[member][:, None] * raw_grad).astype(jnp.bfloat16))
        gate_list.append(jnp.sum(saved_rows[member].astype(jnp.float32) * raw_grad, axis=1))
        scaled = (gate_rows[member][:, None] * grad_rows[member].astype(jnp.float32)).astype(jnp.bfloat16)
        weight_grad = lax.dot_general(saved_rows[member], scaled, (((0,), (0,)), ((), ())), preferred_element_type=jnp.float32)
        summed = summed + jnp.sum(weight_grad * slope_values, axis=0)
    return jnp.stack(hidden_list), jnp.stack(gate_list), summed


def reference(out_grad, routing, gate_codes, hidden_saved, down_weight, channel_scale):
    groups = DATA * SOURCES
    slot_index = slot_places(routing)
    gate_values = gate_codes.reshape(groups, GROUP * 2).astype(jnp.float32) / 256.0
    pair_rows = jnp.repeat(out_grad.reshape(groups, GROUP, D), 2, axis=1)
    group_index = jnp.arange(groups, dtype=jnp.int32)[:, None]
    sent_rows = jnp.zeros((groups, EXPERTS * CAP, D), jnp.bfloat16).at[group_index, slot_index].set(pair_rows)
    sent_gate = jnp.zeros((groups, EXPERTS * CAP), jnp.float32).at[group_index, slot_index].set(gate_values)
    received = sent_rows.reshape(DATA, SOURCES, EXPERTS, CAP, D).transpose(1, 0, 2, 3, 4)
    received = received.transpose(2, 1, 0, 3, 4).reshape(EXPERTS, DATA, SOURCES * CAP, D)
    received_gate = sent_gate.reshape(DATA, SOURCES, EXPERTS, CAP).transpose(2, 0, 1, 3).reshape(EXPERTS, DATA, SOURCES * CAP)
    saved_rows = hidden_saved.reshape(DATA, EXPERTS, SOURCES * CAP, FF).transpose(1, 0, 2, 3)
    hidden_all, gate_all, scale_grad = lax.map(one_expert, (down_weight, channel_scale, received, received_gate, saved_rows))
    hidden_grad = hidden_all.transpose(1, 0, 2, 3).reshape(DATA, EXPERTS, SOURCES, CAP, FF)
    slot_gate = gate_all.reshape(EXPERTS, DATA, SOURCES, CAP).transpose(1, 2, 0, 3).reshape(groups, EXPERTS * CAP)
    gate_grad = jnp.take_along_axis(slot_gate, slot_index, axis=1).reshape(TOKENS, 2)
    return hidden_grad, scale_grad, gate_grad
```

```python
import functools
import math

import jax
import jax.numpy as jnp
from jax import lax
from jax.experimental import pallas as pl
from jax.experimental.pallas import tpu as pltpu
from jax.sharding import PartitionSpec as P

MESH = pl.DeviceIdType.MESH
F32 = jnp.float32
BF16 = jnp.bfloat16
LANES = 128


def remote(src, dst, send_sem, recv_sem, device):
    return pltpu.make_async_remote_copy(
        src_ref=src,
        dst_ref=dst,
        send_sem=send_sem,
        recv_sem=recv_sem,
        device_id=device,
        device_id_type=MESH,
    )


def iota(shape, axis):
    return lax.broadcasted_iota(jnp.int32, shape, axis)


def kernel(
    nt, ne, cap, units, half,
    og, rt, gc, cs, hs, dw,
    hg_out, sg_out, gg_out,
    W, S, HS, QZ, SL, TM, TOKP, SRCP, QT, PMSG, PX, XP, QS, XQ, ACC, GB,
    SPART, SRECV, SX, SY, SALL, GM, GV, PV, PVR,
    lsem, wsem, ssem, zsem, qrsem, qlsem, pxsem, prsem, plsem, xqsem,
    gxsem, gzsem, srsem, sxsem, sasem,
):
    d = lax.axis_index("dp")
    e = lax.axis_index("expert")
    t = lax.axis_index("tensor")
    side = math.isqrt(ne)
    ex, ey = lax.div(e, side), lax.rem(e, side)
    group = 8 * nt
    slots = ne * cap
    phalf = (nt // 2) * LANES
    qhalf = half - phalf
    n_right, n_left = nt // 2, nt // 2 - 1
    other = 1 - d

    def zpeer(k):
        return lax.rem(t + k + nt, nt)

    def xpeer(o):
        return lax.rem(ex + o // side, side) * side + lax.rem(ey + o % side, side)

    partner = (other, e, t)

    load_w = pltpu.make_async_copy(dw, W.at[d], lsem.at[0])
    load_h = pltpu.make_async_copy(hs, HS, lsem.at[1])
    load_w.start()
    load_h.start()

    barrier = pltpu.get_barrier_semaphore()
    pl.semaphore_signal(barrier, inc=1, device_id=partner, device_id_type=MESH)
    for k in range(1, nt):
        pl.semaphore_signal(barrier, inc=1, device_id=(d, e, zpeer(k)), device_id_type=MESH)
    for o in range(1, ne):
        pl.semaphore_signal(barrier, inc=1, device_id=(d, xpeer(o), t), device_id_type=MESH)

    S[d] = jnp.broadcast_to(cs[...].astype(F32), (8, half))
    for j in range(nt):
        start = (j // (nt // 2)) * half + (j % (nt // 2)) * LANES
        SRCP[j] = og[:, start : start + LANES].astype(F32)
    TOKP[t] = SRCP[t]
    QT[t] = jnp.concatenate(
        [og[:, phalf:half].astype(F32), og[:, half + phalf : 2 * half].astype(F32)], axis=0
    ).astype(BF16)

    pl.semaphore_wait(barrier, nt + ne - 1)

    started = []

    def go(copy):
        copy.start()
        started.append(copy)
        return copy

    right, left = (d, e, zpeer(1)), (d, e, zpeer(-1))
    go(remote(QT.at[t], QT.at[t], qrsem.at[0, 1], qrsem.at[1, 1], right))
    go(remote(QT.at[t], QT.at[t], qlsem.at[0, 1], qlsem.at[1, 1], left))
    for k in range(1, nt):
        go(remote(SRCP.at[zpeer(k)], TOKP.at[t], zsem.at[0, k], zsem.at[1, k], (d, e, zpeer(k))))
    go(remote(S.at[d], S.at[d], ssem.at[0], ssem.at[1], partner))
    go(remote(dw, W.at[d], wsem.at[0], wsem.at[1], partner))

    def ring_q(k):
        jr, jl = zpeer(-k), zpeer(k)
        remote(QT.at[jr], QT.at[jr], qrsem.at[0, k], qrsem.at[1, k], right).wait_recv()
        if k < n_right:
            go(remote(QT.at[jr], QT.at[jr], qrsem.at[0, k + 1], qrsem.at[1, k + 1], right))
        if k <= n_left:
            remote(QT.at[jl], QT.at[jl], qlsem.at[0, k], qlsem.at[1, k], left).wait_recv()
            if k < n_left:
                go(remote(QT.at[jl], QT.at[jl], qlsem.at[0, k + 1], qlsem.at[1, k + 1], left))

    wide = 2 * group + group
    column = iota((group, wide), 1)
    token_of = jnp.where(
        column < 2 * group,
        lax.shift_right_logical(column, 4) * 8 + jnp.bitwise_and(column, 7),
        column - 2 * group,
    )
    row = iota((group, wide), 0)
    same = row == token_of
    earlier = jnp.where(row < token_of, 1.0, 0.0).astype(BF16)
    routes = rt[...].astype(F32)
    codes = gc[...].astype(F32)
    name = [jnp.sum(jnp.where(same, routes[:, k : k + 1], 0.0), axis=0, keepdims=True) for k in (0, 1)]
    gate = [
        jnp.sum(jnp.where(same, codes[:, k : k + 1], 0.0), axis=0, keepdims=True)[:, 2 * group :]
        for k in (0, 1)
    ]
    expert_row = iota((ne, wide), 0).astype(F32)
    names = [jnp.where(expert_row == name[k], 1.0, 0.0) for k in (0, 1)]
    both = (names[0] + names[1])[:, 2 * group :].astype(BF16)
    before = jnp.dot(both, earlier, preferred_element_type=F32)
    place = [jnp.sum(names[k] * before, axis=0, keepdims=True) for k in (0, 1)]
    slot = [name[k] * float(cap) + place[k] for k in (0, 1)]
    slot_row = iota((slots, wide), 0).astype(F32)
    picks = [jnp.where(slot_row == slot[k], 1.0, 0.0) for k in (0, 1)]
    pick = picks[0] + picks[1]
    pick_p = pick[:, 2 * group :].astype(BF16)
    in_half = jnp.bitwise_and(lax.shift_right_logical(iota((slots, 2 * group), 1), 3), 1)
    pick_q = [jnp.where(in_half == a, pick[:, : 2 * group], 0.0).astype(BF16) for a in (0, 1)]
    gate_pick = (
        picks[0][:, 2 * group :] * gate[0] + picks[1][:, 2 * group :] * gate[1]
    ).astype(BF16)
    gates = jnp.dot(gate_pick, jnp.ones((group, LANES), BF16), preferred_element_type=F32)
    gates = (gates * (1.0 / 256.0)).astype(BF16)

    ring_q(1)

    for k in range(1, nt):
        remote(SRCP.at[t], TOKP.at[zpeer(-k)], zsem.at[0, k], zsem.at[1, k], right).wait_recv()
    tokens = TOKP[...].reshape(group, LANES).astype(BF16)
    routed = jnp.dot(pick_p, tokens, preferred_element_type=F32).astype(BF16)
    PMSG[:, :cap, :] = routed.reshape(ne, cap, LANES)
    PMSG[:, cap:, :] = gates.reshape(ne, cap, LANES)
    PX[e] = PMSG[e]
    for o in range(1, ne):
        go(remote(PMSG.at[xpeer(o)], PX.at[e], pxsem.at[0, o], pxsem.at[1, o], (d, xpeer(o), t)))

    load_w.wait()
    load_h.wait()

    def unit(hh, block):
        lanes = slice(block * 256, block * 256 + 256)
        scale = S[hh, 0:1, lanes]
        inverse = 1.0 / scale

        def rows(i, carry):
            at = pl.ds(pl.multiple_of(i * 128, 128), 128)
            u = W[hh, at, lanes].astype(F32) * inverse
            b = jnp.tanh(u)
            QZ[hh, at, lanes] = (scale * b).astype(BF16)
            SL[at, :] = (b - u * (1.0 - b * b)).astype(BF16)
            return carry

        lax.fori_loop(0, units // 128, rows, 0)
        TM[hh, :, lanes] = jnp.dot(HS[...], SL[...], preferred_element_type=F32)

    n_units = half // 256
    work = [(d, b) for b in range(n_units)]
    work_other = [(other, b) for b in range(n_units)]

    def do(n):
        for _ in range(n):
            if work:
                unit(*work.pop(0))

    ring_q(2)
    do(1)
    for k in range(3, n_right):
        ring_q(k)
        if k == n_right - 3:
            pass
        do(1)
    for o in range(1, ne):
        remote(PMSG.at[e], PX.at[xpeer(ne - o)], pxsem.at[0, o], pxsem.at[1, o], right).wait_recv()
    XP[t] = PX[:, :cap, :].reshape(slots, LANES)
    GB[...] = PX[:, cap:, :].reshape(slots, LANES).astype(F32)
    pieces = 2
    prow = slots // pieces

    def piece(j, i):
        return XP.at[j, pl.ds(i * prow, prow)]

    for i in range(pieces):
        go(remote(piece(t, i), piece(t, i), prsem.at[0, 1, i], prsem.at[1, 1, i], right))
        go(remote(piece(t, i), piece(t, i), plsem.at[0, 1, i], plsem.at[1, 1, i], left))

    def ring_p(k):
        jr, jl = zpeer(-k), zpeer(k)
        for i in range(pieces):
            remote(piece(jr, i), piece(jr, i), prsem.at[0, k, i], prsem.at[1, k, i], right).wait_recv()
            if k < n_right:
                go(remote(piece(jr, i), piece(jr, i), prsem.at[0, k + 1, i], prsem.at[1, k + 1, i], right))
            if k <= n_left:
                remote(piece(jl, i), piece(jl, i), plsem.at[0, k, i], plsem.at[1, k, i], left).wait_recv()
                if k < n_left:
                    go(remote(piece(jl, i), piece(jl, i), plsem.at[0, k + 1, i], plsem.at[1, k + 1, i], left))

    if n_right > 2:
        ring_q(n_right)

    for a in (0, 1):
        gathered = QT[...].reshape(2 * group, qhalf)
        step = 256
        for c in range(0, qhalf, step):
            QS[a, :, :, c : c + step] = (
                jnp.dot(pick_q[a], gathered[:, c : c + step], preferred_element_type=F32)
                .astype(BF16)
                .reshape(ne, cap, step)
            )
        for o in range(1, ne):
            go(remote(QS.at[a, xpeer(o)], XQ.at[a, e], xqsem.at[0, a, o], xqsem.at[1, a, o], (d, xpeer(o), t)))
        XQ[a, e] = QS[a, e]

    ACC[...] = jnp.zeros_like(ACC)

    def terms(x, hh, start):
        scaled = (x.astype(F32) * GB[...]).astype(BF16).astype(F32)
        return jnp.sum(scaled * TM[hh, :, pl.ds(start, LANES)], axis=0, keepdims=True)

    def chunk_p(js):
        xs, qs = [], []
        for j in js:
            hh = lax.div(j, nt // 2)
            b = lax.rem(j, nt // 2)
            start = pl.multiple_of(b * LANES, LANES)
            x = XP[j]
            SPART[b, pl.ds(hh, 1), :] = terms(x, hh, start)
            xs.append(x)
            qs.append(QZ[hh, :, pl.ds(start, LANES)])
        x = xs[0] if len(xs) == 1 else jnp.concatenate(xs, axis=1)
        q = qs[0] if len(qs) == 1 else jnp.concatenate(qs, axis=1)
        ACC[...] += lax.dot_general(x, q, (((1,), (1,)), ((), ())), preferred_element_type=F32)

    ring_p(1)
    do(n_units)
    remote(S.at[d], S.at[other], ssem.at[0], ssem.at[1], partner).wait_recv()
    remote(dw, W.at[other], wsem.at[0], wsem.at[1], partner).wait_recv()
    work.extend(work_other)
    per = -(-n_units // 4)
    for k in range(2, 6):
        if k <= n_right:
            ring_p(k)
        do(per)
    do(n_units)
    chunk_p([t])
    for k in range(1, min(5, n_right)):
        chunk_p([zpeer(-k), zpeer(k)])
    for k in range(6, n_right + 1):
        ring_p(k)
        chunk_p([zpeer(1 - k), zpeer(k - 1)])
    if n_right >= 2 and n_right < 6:
        chunk_p([zpeer(1 - n_right), zpeer(n_right - 1)]) if n_right == 5 else None
    chunk_p([zpeer(n_right)])

    def send_terms(k):
        go(remote(SPART.at[zpeer(k)], SRECV.at[t], srsem.at[0, k], srsem.at[1, k], (d, e, zpeer(k))))

    for a in (0, 1):
        for o in range(1, ne):
            remote(QS.at[a, e], XQ.at[a, xpeer(ne - o)], xqsem.at[0, a, o], xqsem.at[1, a, o], right).wait_recv()
        for c in range(0, qhalf, LANES):
            x = XQ[a, :, :, c : c + LANES].reshape(slots, LANES)
            SPART[nt // 2 + c // LANES, a : a + 1, :] = terms(x, a, phalf + c)
        if a == 1:
            SRECV[t] = SPART[t]
            for k in range(1, nt):
                send_terms(k)
        ACC[...] += lax.dot_general(
            XQ[a].reshape(slots, qhalf),
            QZ[a, :, phalf:half],
            (((1,), (1,)), ((), ())),
            preferred_element_type=F32,
        )

    weighed = ACC[:, 0:LANES] * HS[:, 0:LANES].astype(F32)
    for c in range(LANES, units, LANES):
        weighed += ACC[:, c : c + LANES] * HS[:, c : c + LANES].astype(F32)
    weighed = jnp.sum(weighed, axis=1, keepdims=True)
    at_place = jnp.bitwise_and(iota((slots, LANES), 0), cap - 1) == iota((slots, LANES), 1)
    GM[...] = jnp.sum(
        jnp.where(at_place, weighed, 0.0).reshape(ne, cap, LANES), axis=1, keepdims=True
    )
    GV[e] = GM[e]
    for o in range(1, ne):
        go(remote(GM.at[xpeer(o)], GV.at[e], gxsem.at[0, o], gxsem.at[1, o], (d, xpeer(o), t)))

    for k in range(1, nt):
        remote(SPART.at[t], SRECV.at[zpeer(-k)], srsem.at[0, k], srsem.at[1, k], right).wait_recv()
    total = SRECV[0]
    for i in range(1, nt):
        total += SRECV[i]
    SX[0] = total[0:1]
    SX[1] = total[1:2]
    go(remote(SX.at[other], SY, sxsem.at[0], sxsem.at[1], partner))

    for c in range(0, units, LANES):
        hg_out[:, c : c + LANES] = (ACC[:, c : c + LANES] * GB[...]).astype(BF16)

    remote(SX.at[d], SY, sxsem.at[0], sxsem.at[1], partner).wait_recv()
    SALL[t] = SX[d] + SY[...]
    for k in range(1, nt):
        go(remote(SALL.at[t], SALL.at[t], sasem.at[0, k], sasem.at[1, k], (d, e, zpeer(k))))

    for o in range(1, ne):
        remote(GM.at[e], GV.at[xpeer(ne - o)], gxsem.at[0, o], gxsem.at[1, o], right).wait_recv()
    values = jnp.concatenate([GV[i] for i in range(ne)], axis=0)
    place_row = iota((LANES, group), 0).astype(F32)
    pair_rows = []
    for k in (0, 1):
        chosen = jnp.where(place_row == place[k][:, 2 * group :], 1.0, 0.0)
        spread = jnp.dot(values, chosen, precision=lax.Precision.HIGHEST, preferred_element_type=F32)
        pair_rows.append(jnp.sum(spread * names[k][:, 2 * group :], axis=0, keepdims=True))
    PV[...] = jnp.concatenate(pair_rows, axis=0)
    PVR[t] = PV[...]
    for k in range(1, nt):
        go(remote(PV, PVR.at[t], gzsem.at[0, k], gzsem.at[1, k], (d, e, zpeer(k))))

    for k in range(1, nt):
        remote(SALL.at[t], SALL.at[zpeer(-k)], sasem.at[0, k], sasem.at[1, k], right).wait_recv()
    for i in range(nt):
        sg_out[:, i * LANES : (i + 1) * LANES] = SALL[i]

    for k in range(1, nt):
        remote(PV, PVR.at[zpeer(-k)], gzsem.at[0, k], gzsem.at[1, k], right).wait_recv()
    total = PVR[0]
    for i in range(1, nt):
        total += PVR[i]
    mine = iota((8, group), 1) == t * 8 + iota((8, group), 0)
    pair = [jnp.sum(jnp.where(mine, total[k : k + 1], 0.0), axis=1, keepdims=True) for k in (0, 1)]
    gg_out[...] = jnp.concatenate(pair, axis=1)

    for copy in started:
        copy.wait_send()


def on_device(nt, ne, out_grad, routing, gate_codes, hidden_saved, down_weight, channel_scale):
    cap = hidden_saved.shape[3]
    units = hidden_saved.shape[4]
    half = down_weight.shape[2]
    group = routing.shape[0]
    slots = ne * cap
    phalf = (nt // 2) * LANES
    qhalf = half - phalf
    vmem = pl.BlockSpec(memory_space=pltpu.VMEM)
    anywhere = pl.BlockSpec(memory_space=pl.ANY)
    dma = pltpu.SemaphoreType.DMA
    hidden_grad, scale_grad, gate_grad = pl.pallas_call(
        functools.partial(kernel, nt, ne, cap, units, half),
        out_shape=(
            jax.ShapeDtypeStruct((slots, units), BF16),
            jax.ShapeDtypeStruct((1, half), F32),
            jax.ShapeDtypeStruct((8, 2), F32),
        ),
        in_specs=[vmem, vmem, vmem, vmem, anywhere, anywhere],
        out_specs=(vmem, vmem, vmem),
        scratch_shapes=[
            pltpu.VMEM((2, units, half), BF16),
            pltpu.VMEM((2, 8, half), F32),
            pltpu.VMEM((slots, units), BF16),
            pltpu.VMEM((2, units, half), BF16),
            pltpu.VMEM((units, 256), BF16),
            pltpu.VMEM((2, slots, half), F32),
            pltpu.VMEM((nt, 8, LANES), F32),
            pltpu.VMEM((nt, 8, LANES), F32),
            pltpu.VMEM((nt, 16, qhalf), BF16),
            pltpu.VMEM((ne, 2 * cap, LANES), BF16),
            pltpu.VMEM((ne, 2 * cap, LANES), BF16),
            pltpu.VMEM((nt, slots, LANES), BF16),
            pltpu.VMEM((2, ne, cap, qhalf), BF16),
            pltpu.VMEM((2, ne, cap, qhalf), BF16),
            pltpu.VMEM((slots, units), F32),
            pltpu.VMEM((slots, LANES), F32),
            pltpu.VMEM((nt, 2, LANES), F32),
            pltpu.VMEM((nt, 2, LANES), F32),
            pltpu.VMEM((2, 1, LANES), F32),
            pltpu.VMEM((1, LANES), F32),
            pltpu.VMEM((nt, 1, LANES), F32),
            pltpu.VMEM((ne, 1, LANES), F32),
            pltpu.VMEM((ne, 1, LANES), F32),
            pltpu.VMEM((2, LANES if group == LANES else group), F32),
            pltpu.VMEM((nt, 2, group), F32),
            dma((2,)),
            dma((2,)),
            dma((2,)),
            dma((2, nt)),
            dma((2, nt // 2 + 1)),
            dma((2, nt // 2 + 1)),
            dma((2, ne)),
            dma((2, nt // 2 + 1, 2)),
            dma((2, nt // 2 + 1, 2)),
            dma((2, 2, ne)),
            dma((2, ne)),
            dma((2, nt)),
            dma((2, nt)),
            dma((2,)),
            dma((2, nt)),
        ],
        compiler_params=pltpu.CompilerParams(
            collective_id=0, has_side_effects=True, vmem_limit_bytes=60 * 1024 * 1024
        ),
    )(
        out_grad,
        routing,
        gate_codes,
        channel_scale,
        hidden_saved.reshape(slots, units),
        down_weight.reshape(units, half),
    )
    return hidden_grad.reshape(hidden_saved.shape), scale_grad, gate_grad


def solution(mesh):
    in_specs = (
        P(("dp", "expert", "tensor"), None),
        P(("dp", "expert"), None),
        P(("dp", "expert"), None),
        P("dp", "expert", None, None, "tensor"),
        P("expert", "tensor", "dp"),
        P("expert", "dp"),
    )
    out_specs = (
        P("dp", "expert", None, None, "tensor"),
        P("expert", "dp"),
        P(("dp", "expert", "tensor"), None),
    )
    return jax.shard_map(
        functools.partial(on_device, mesh.shape["tensor"], mesh.shape["expert"]),
        mesh=mesh,
        in_specs=in_specs,
        out_specs=out_specs,
        check_vma=False,
    )
```

```python
import functools
import math

import jax
import jax.numpy as jnp
from jax import lax
from jax.experimental import pallas as pl
from jax.experimental.pallas import tpu as pltpu
from jax.sharding import PartitionSpec as P

MESH = pl.DeviceIdType.MESH
F32 = jnp.float32
BF16 = jnp.bfloat16
LANES = 128


def remote(src, dst, send_sem, recv_sem, device):
    return pltpu.make_async_remote_copy(
        src_ref=src,
        dst_ref=dst,
        send_sem=send_sem,
        recv_sem=recv_sem,
        device_id=device,
        device_id_type=MESH,
    )


def iota(shape, axis):
    return lax.broadcasted_iota(jnp.int32, shape, axis)


def gather_plan(nt):
    if nt == 16:
        return {0: (8, 4, -4, 1, -1, 2, -2), -4: (1, -1, 2), 4: (1, -1, -2), 8: (1, -1)}
    return {0: tuple(range(1, nt))}


def kernel(
    nt, ne, cap, units, half,
    og, rt, gc, cs, hs, dw,
    hg_out, sg_out, gg_out,
    W, S, HS, QZ, SL, TM, TOKP, SRCP, QT, PMSG, PX, XP, QS, XQ, ACC, GB, HG,
    SPART, SPX, SSUM, SRECV, GM, GV, PV, PVR,
    lsem, wsem, ssem, zsem, qasem, qbsem, pxsem, prsem, psend, xqsem,
    gxsem, gzsem, spsem, srsem,
):
    d = lax.axis_index("dp")
    e = lax.axis_index("expert")
    t = lax.axis_index("tensor")
    side = math.isqrt(ne)
    ex, ey = lax.div(e, side), lax.rem(e, side)
    group = 8 * nt
    slots = ne * cap
    n_chunks = nt // 2
    chunk_w = 2 * LANES
    per_half = n_chunks // 2
    phalf = per_half * chunk_w
    qhalf = half - phalf
    part = qhalf // 2
    blocks = half // LANES
    reach = n_chunks // 2
    other = 1 - d

    def zpeer(k):
        return lax.rem(t + k + nt, nt)

    def xpeer(o):
        return lax.rem(ex + o // side, side) * side + lax.rem(ey + o % side, side)

    def at_z(k):
        return (d, e, zpeer(k))

    def at_x(o):
        return (d, xpeer(o), t)

    partner = (other, e, t)
    right, left = at_z(1), at_z(-1)

    def arrived(ref, sems):
        remote(ref, ref, sems.at[0], sems.at[1], partner).wait_recv()

    def left_here(ref, sems):
        remote(ref, ref, sems.at[0], sems.at[1], partner).wait_send()

    load_w = pltpu.make_async_copy(dw, W.at[d], lsem.at[0])
    load_h = pltpu.make_async_copy(hs, HS, lsem.at[1])
    load_w.start()
    load_h.start()

    barrier = pltpu.get_barrier_semaphore()
    for k in range(1, nt):
        pl.semaphore_signal(barrier, inc=1, device_id=at_z(k), device_id_type=MESH)
    for o in range(1, ne):
        pl.semaphore_signal(barrier, inc=1, device_id=at_x(o), device_id_type=MESH)
    pl.semaphore_signal(barrier, inc=1, device_id=partner, device_id_type=MESH)

    def two_rows(first, second, width):
        upper = og[:, first : first + width].astype(F32)
        lower = og[:, second : second + width].astype(F32)
        return jnp.concatenate([upper, lower], axis=0).astype(BF16)

    for i in (0, 1):
        QT[i, t] = two_rows(phalf + i * part, half + phalf + i * part, part)
    for j in range(n_chunks):
        start = (j // per_half) * half + (j % per_half) * chunk_w
        SRCP[j] = two_rows(start, start + LANES, LANES)
    TOKP[t] = SRCP[lax.rem(t, n_chunks)]
    S[d] = jnp.broadcast_to(cs[...].astype(F32), (8, half))

    pl.semaphore_wait(barrier, nt + ne - 1)

    plan = gather_plan(nt)
    via = [rel for rel in plan if rel]

    def send_tokens(i, rel, offsets):
        chunk = QT.at[i, zpeer(rel)]
        for k in offsets:
            seen = -k if k != 8 else 8
            recv = qasem.at[i, via.index(seen)] if rel == 0 and seen in via else qbsem.at[i, 1]
            remote(chunk, chunk, qbsem.at[i, 0], recv, at_z(k)).start()

    def tokens_from(i, rel):
        chunk = QT.at[i, zpeer(rel)]
        remote(chunk, chunk, qbsem.at[i, 0], qasem.at[i, via.index(rel)], partner).wait_recv()
        send_tokens(i, rel, plan[rel])

    send_tokens(0, 0, plan[0][:3])
    for k in range(1, nt):
        source = SRCP.at[lax.rem(zpeer(k), n_chunks)]
        remote(source, TOKP.at[t], zsem.at[0], zsem.at[1], at_z(k)).start()
    send_tokens(0, 0, plan[0][3:])
    send_tokens(1, 0, plan[0])
    remote(S.at[d], S.at[d], ssem.at[0], ssem.at[1], partner).start()
    remote(dw, W.at[d], wsem.at[0], wsem.at[1], partner).start()

    wide = 2 * group + group
    column = iota((group, wide), 1)
    token_of = jnp.where(
        column < 2 * group,
        lax.shift_right_logical(column, 4) * 8 + jnp.bitwise_and(column, 7),
        column - 2 * group,
    )
    row = iota((group, wide), 0)
    same = jnp.where(row == token_of, 1.0, 0.0).astype(BF16)
    earlier = jnp.where(row < token_of, 1.0, 0.0).astype(BF16)
    routes = jnp.dot(rt[...].astype(F32).astype(BF16), same, preferred_element_type=F32)
    codes = gc[...].astype(F32)
    name = [routes[k : k + 1] for k in (0, 1)]
    gate = [codes[k : k + 1] for k in (0, 1)]
    expert_row = iota((ne, wide), 0).astype(F32)
    names = [jnp.where(expert_row == name[k], 1.0, 0.0) for k in (0, 1)]
    both = (names[0] + names[1])[:, 2 * group :].astype(BF16)
    before = jnp.dot(both, earlier, preferred_element_type=F32)
    place = [jnp.sum(names[k] * before, axis=0, keepdims=True) for k in (0, 1)]
    slot = [name[k] * float(cap) + place[k] for k in (0, 1)]
    slot_row = iota((slots, wide), 0).astype(F32)
    picks = [jnp.where(slot_row == slot[k], 1.0, 0.0) for k in (0, 1)]
    pick = picks[0] + picks[1]
    in_half = jnp.bitwise_and(lax.shift_right_logical(iota((slots, 2 * group), 1), 3), 1)
    pick_q = [jnp.where(in_half == a, pick[:, : 2 * group], 0.0).astype(BF16) for a in (0, 1)]
    gate_pick = (
        picks[0][:, 2 * group :] * gate[0] + picks[1][:, 2 * group :] * gate[1]
    ).astype(BF16)
    gates = jnp.dot(gate_pick, jnp.ones((group, LANES), BF16), preferred_element_type=F32)
    PMSG[:, 2 * cap :, :] = (gates * (1.0 / 256.0)).astype(BF16).reshape(ne, cap, LANES)

    load_w.wait()
    load_h.wait()

    def unit(hh, block):
        lanes = slice(block * 256, block * 256 + 256)
        scale = S[hh, 0:1, lanes]
        inverse = 1.0 / scale

        def rows(i, carry):
            at = pl.ds(pl.multiple_of(i * 128, 128), 128)
            u = W[hh, at, lanes].astype(F32) * inverse
            b = jnp.tanh(u)
            QZ[hh, at, lanes] = (scale * b).astype(BF16)
            SL[at, :] = (b - u * (1.0 - b * b)).astype(BF16)
            return carry

        lax.fori_loop(0, units // 128, rows, 0)
        TM[hh, :, lanes] = jnp.dot(HS[...], SL[...], preferred_element_type=F32)

    def partner_ready():
        arrived(S.at[other], ssem)
        arrived(W.at[other], wsem)

    def terms(x, hh, start):
        scaled = (x.astype(F32) * GB[...]).astype(BF16).astype(F32)
        return jnp.sum(scaled * TM[hh, :, pl.ds(start, LANES)], axis=0, keepdims=True)

    def chunk_p(j):
        hh = lax.div(j, per_half)
        b = lax.rem(j, per_half)
        start = pl.multiple_of(b * chunk_w, chunk_w)
        for i in (0, 1):
            x = XP[j, :, i * LANES : (i + 1) * LANES]
            SPART[hh, 2 * b + i] = terms(x, hh, pl.multiple_of(start + i * LANES, LANES))
        ACC[...] += lax.dot_general(
            XP[j],
            QZ[hh, :, pl.ds(start, chunk_w)],
            (((1,), (1,)), ((), ())),
            preferred_element_type=F32,
        )

    def parts_q(i):
        arrived(XQ.at[i, pl.ds(0, ne - 1)], xqsem.at[i])
        for a in (0, 1):
            for c in range(part // LANES):
                at = i * part + c * LANES
                x = XQ[i, :, :, a * part + c * LANES : a * part + (c + 1) * LANES]
                SPART[a, (phalf + at) // LANES] = terms(x.reshape(slots, LANES), a, phalf + at)

    def dot_q(i):
        for a in (0, 1):
            ACC[...] += lax.dot_general(
                XQ[i, :, :, a * part : (a + 1) * part].reshape(slots, part),
                QZ[a, :, phalf + i * part : phalf + (i + 1) * part],
                (((1,), (1,)), ((), ())),
                preferred_element_type=F32,
            )

    pb, qb = phalf // 256, qhalf // 256
    work = [functools.partial(unit, d, b) for b in range(pb)]
    work += [partner_ready]
    work += [functools.partial(unit, other, b) for b in range(pb)]
    work += [functools.partial(unit, h, pb + b) for b in range(qb) for h in (d, other)]
    chunks = [functools.partial(chunk_p, lax.rem(t, n_chunks))]
    for k in range(1, reach):
        for rel in (-k, k):
            chunks += [functools.partial(chunk_p, lax.rem(zpeer(rel), n_chunks))]
    chunks += [functools.partial(chunk_p, lax.rem(zpeer(reach), n_chunks))]

    def do(jobs, n):
        for _ in range(n):
            if jobs:
                jobs.pop(0)()


    do(work, 2)
    for rel in via[:2]:
        tokens_from(0, rel)

    arrived(TOKP.at[pl.ds(0, nt - 1)], zsem)
    tokens = TOKP[...].reshape(2 * group, LANES)
    for a in (0, 1):
        routed = jnp.dot(pick_q[a], tokens, preferred_element_type=F32).astype(BF16)
        PMSG[:, a * cap : (a + 1) * cap, :] = routed.reshape(ne, cap, LANES)
    for o in range(1, ne):
        remote(PMSG.at[xpeer(o)], PX.at[e], pxsem.at[0], pxsem.at[1], at_x(o)).start()
    PX[e] = PMSG[e]

    for rel in via[2:]:
        tokens_from(0, rel)
    for rel in via:
        tokens_from(1, rel)
    do(work, 2)

    n_direct = nt - 1 - len(via)

    def route_q(i):
        arrived(QT.at[i, pl.ds(0, n_direct)], qbsem.at[i])
        gathered = QT[i].reshape(2 * group, part)
        step = min(256, part)
        for a in (0, 1):
            for c in range(0, part, step):
                QS[i, :, :, a * part + c : a * part + c + step] = (
                    jnp.dot(pick_q[a], gathered[:, c : c + step], preferred_element_type=F32)
                    .astype(BF16)
                    .reshape(ne, cap, step)
                )
        for o in range(1, ne):
            remote(QS.at[i, xpeer(o)], XQ.at[i, e], xqsem.at[i, 0], xqsem.at[i, 1], at_x(o)).start()
        XQ[i, e] = QS[i, e]

    route_q(0)

    pieces = 4
    prow = slots // pieces

    def piece(j, i):
        return XP.at[j, pl.ds(i * prow, prow)]

    def pass_on(way, rel, k, i):
        if k == reach and (i < pieces // 2) != (way == 0):
            return
        ref = piece(lax.rem(zpeer(rel), n_chunks), i)
        remote(ref, ref, psend.at[way], prsem.at[way, k, i], (right, left)[way]).start()

    def ring_p(k):
        for i in range(pieces):
            for way in (0, 1):
                if k == reach and (i < pieces // 2) != (way == 0):
                    continue
                rel = -k if way == 0 else k
                ref = piece(lax.rem(zpeer(rel), n_chunks), i)
                remote(ref, ref, psend.at[way], prsem.at[way, k, i], partner).wait_recv()
                if k < reach:
                    pass_on(way, rel, k + 1, i)

    arrived(PX.at[pl.ds(0, ne - 1)], pxsem)
    mine_p = lax.rem(t, n_chunks)
    for a in (0, 1):
        XP[mine_p, :, a * LANES : (a + 1) * LANES] = PX[:, a * cap : (a + 1) * cap, :].reshape(slots, LANES)
    for i in range(pieces):
        for way in (0, 1):
            pass_on(way, 0, 1, i)
    GB[...] = PX[:, 2 * cap :, :].reshape(slots, LANES).astype(F32)
    ACC[...] = jnp.zeros_like(ACC)
    route_q(1)

    do(work, 2)
    for k in range(1, reach):
        ring_p(k)
        do(work, -(-len(work) // (reach - k)))
        if k == reach - 1:
            do(chunks, 2 * reach - 3)
        elif k > 1:
            do(chunks, 2)
    do(work, len(work))
    parts_q(0)
    dot_q(0)
    ring_p(reach)
    do(chunks, len(chunks))
    parts_q(1)
    remote(SPART.at[other], SPX, spsem.at[0], spsem.at[1], partner).start()
    dot_q(1)

    weighed = ACC[:, 0:LANES] * HS[:, 0:LANES].astype(F32)
    for c in range(LANES, units, LANES):
        weighed += ACC[:, c : c + LANES] * HS[:, c : c + LANES].astype(F32)
    weighed = jnp.sum(weighed, axis=1, keepdims=True)
    at_place = jnp.bitwise_and(iota((slots, LANES), 0), cap - 1) == iota((slots, LANES), 1)
    GM[...] = jnp.sum(
        jnp.where(at_place, weighed, 0.0).reshape(ne, cap, LANES), axis=1, keepdims=True
    )
    for o in range(1, ne):
        remote(GM.at[xpeer(o)], GV.at[e], gxsem.at[0], gxsem.at[1], at_x(o)).start()
    GV[e] = GM[e]

    arrived(SPX, spsem)
    SSUM[...] = SPART[d] + SPX[...]
    for k in range(1, nt):
        remote(SSUM, SRECV.at[t], srsem.at[0], srsem.at[1], at_z(k)).start()
    SRECV[t] = SSUM[...]

    for c in range(0, units, LANES):
        HG[:, c : c + LANES] = (ACC[:, c : c + LANES] * GB[...]).astype(BF16)
    save = pltpu.make_async_copy(HG, hg_out, lsem.at[0])
    save.start()

    arrived(GV.at[pl.ds(0, ne - 1)], gxsem)
    values = jnp.concatenate([GV[i] for i in range(ne)], axis=0)
    place_row = iota((LANES, group), 0).astype(F32)
    pair_rows = []
    for k in (0, 1):
        chosen = jnp.where(place_row == place[k][:, 2 * group :], 1.0, 0.0)
        spread = jnp.dot(values, chosen, precision=lax.Precision.HIGHEST, preferred_element_type=F32)
        pair_rows.append(jnp.sum(spread * names[k][:, 2 * group :], axis=0, keepdims=True))
    PV[...] = jnp.concatenate(pair_rows, axis=0)
    for k in range(1, nt):
        remote(PV, PVR.at[t], gzsem.at[0], gzsem.at[1], at_z(k)).start()
    PVR[t] = PV[...]

    arrived(SRECV.at[pl.ds(0, nt - 1)], srsem)
    total = SRECV[0]
    for i in range(1, nt):
        total += SRECV[i]
    for i in range(blocks):
        sg_out[:, i * LANES : (i + 1) * LANES] = total[i]

    arrived(PVR.at[pl.ds(0, nt - 1)], gzsem)
    total = PVR[0]
    for i in range(1, nt):
        total += PVR[i]
    mine = jnp.where(iota((group, 8), 0) == t * 8 + iota((group, 8), 1), 1.0, 0.0)
    gg_out[...] = jnp.dot(total, mine, precision=lax.Precision.HIGHEST, preferred_element_type=F32)

    left_here(TOKP.at[pl.ds(0, nt - 1)], zsem)
    left_here(S.at[d], ssem)
    left_here(dw, wsem)
    left_here(PMSG.at[pl.ds(0, ne - 1)], pxsem)
    for i in (0, 1):
        left_here(QT.at[i, pl.ds(0, nt - 1)], qbsem.at[i])
        left_here(QS.at[i, pl.ds(0, ne - 1)], xqsem.at[i])
    for way in (0, 1):
        ref = XP.at[pl.ds(0, 2 * reach - 1), pl.ds(0, slots // 2)]
        remote(ref, ref, psend.at[way], prsem.at[way, 1, 0], partner).wait_send()
    left_here(GM.at[pl.ds(0, ne - 1)], gxsem)
    left_here(PVR.at[pl.ds(0, nt - 1)], gzsem)
    left_here(SPX, spsem)
    left_here(SRECV.at[pl.ds(0, nt - 1)], srsem)
    save.wait()


def write_kernel(hg, sg, gg, hg_out, sg_out, gg_out):
    hg_out[...] = hg[...]
    sg_out[...] = sg[...]
    gg_out[...] = gg[...]


def on_device(nt, ne, out_grad, routing, gate_codes, hidden_saved, down_weight, channel_scale):
    cap = hidden_saved.shape[3]
    units = hidden_saved.shape[4]
    half = down_weight.shape[2]
    group = routing.shape[0]
    slots = ne * cap
    n_chunks = nt // 2
    qhalf = half - n_chunks * LANES
    blocks = half // LANES
    vmem = pl.BlockSpec(memory_space=pltpu.VMEM)
    anywhere = pl.BlockSpec(memory_space=pl.ANY)
    dma = pltpu.SemaphoreType.DMA
    results = (
        jax.ShapeDtypeStruct((slots, units), BF16),
        jax.ShapeDtypeStruct((1, half), F32),
        jax.ShapeDtypeStruct((2, 8), F32),
    )
    parts = pl.pallas_call(
        functools.partial(kernel, nt, ne, cap, units, half),
        out_shape=results,
        in_specs=[vmem, vmem, vmem, vmem, anywhere, anywhere],
        out_specs=(anywhere, vmem, vmem),
        scratch_shapes=[
            pltpu.VMEM((2, units, half), BF16),
            pltpu.VMEM((2, 8, half), F32),
            pltpu.VMEM((slots, units), BF16),
            pltpu.VMEM((2, units, half), BF16),
            pltpu.VMEM((units, 256), BF16),
            pltpu.VMEM((2, slots, half), F32),
            pltpu.VMEM((nt, 16, LANES), BF16),
            pltpu.VMEM((n_chunks, 16, LANES), BF16),
            pltpu.VMEM((2, nt, 16, qhalf // 2), BF16),
            pltpu.VMEM((ne, 3 * cap, LANES), BF16),
            pltpu.VMEM((ne, 3 * cap, LANES), BF16),
            pltpu.VMEM((n_chunks, slots, 2 * LANES), BF16),
            pltpu.VMEM((2, ne, cap, qhalf), BF16),
            pltpu.VMEM((2, ne, cap, qhalf), BF16),
            pltpu.VMEM((slots, units), F32),
            pltpu.VMEM((slots, LANES), F32),
            pltpu.VMEM((slots, units), BF16),
            pltpu.VMEM((2, blocks, 1, LANES), F32),
            pltpu.VMEM((blocks, 1, LANES), F32),
            pltpu.VMEM((blocks, 1, LANES), F32),
            pltpu.VMEM((nt, blocks, 1, LANES), F32),
            pltpu.VMEM((ne, 1, LANES), F32),
            pltpu.VMEM((ne, 1, LANES), F32),
            pltpu.VMEM((2, group), F32),
            pltpu.VMEM((nt, 2, group), F32),
            dma((2,)),
            dma((2,)),
            dma((2,)),
            dma((2,)),
            dma((2, 3)),
            dma((2, 2)),
            dma((2,)),
            dma((2, n_chunks // 2 + 1, 4)),
            dma((2,)),
            dma((2, 2)),
            dma((2,)),
            dma((2,)),
            dma((2,)),
            dma((2,)),
        ],
        compiler_params=pltpu.CompilerParams(
            collective_id=0, has_side_effects=True, vmem_limit_bytes=60 * 1024 * 1024
        ),
    )(
        out_grad,
        routing.T,
        gate_codes.T,
        channel_scale,
        hidden_saved.reshape(slots, units),
        down_weight.reshape(units, half),
    )
    steps = 4
    tall = pl.BlockSpec((slots // steps, units), lambda i: (i, 0))
    flat = pl.BlockSpec((1, half), lambda i: (0, 0))
    pairs = pl.BlockSpec((2, 8), lambda i: (0, 0))
    hidden_grad, scale_grad, gate_grad = pl.pallas_call(
        write_kernel,
        out_shape=results,
        grid=(steps,),
        in_specs=[tall, flat, pairs],
        out_specs=(tall, flat, pairs),
    )(*parts)
    return hidden_grad.reshape(hidden_saved.shape), scale_grad, gate_grad.T


def solution(mesh):
    in_specs = (
        P(("dp", "expert", "tensor"), None),
        P(("dp", "expert"), None),
        P(("dp", "expert"), None),
        P("dp", "expert", None, None, "tensor"),
        P("expert", "tensor", "dp"),
        P("expert", "dp"),
    )
    out_specs = (
        P("dp", "expert", None, None, "tensor"),
        P("expert", "dp"),
        P(("dp", "expert", "tensor"), None),
    )
    return jax.shard_map(
        functools.partial(on_device, mesh.shape["tensor"], mesh.shape["expert"]),
        mesh=mesh,
        in_specs=in_specs,
        out_specs=out_specs,
        check_vma=False,
    )
```

```python
import functools
import math

import jax
import jax.numpy as jnp
from jax import lax
from jax.experimental import pallas as pl
from jax.experimental.pallas import tpu as pltpu
from jax.sharding import PartitionSpec as P

MESH = pl.DeviceIdType.MESH
F32 = jnp.float32
BF16 = jnp.bfloat16
LANES = 128


def remote(src, dst, send_sem, recv_sem, device):
    return pltpu.make_async_remote_copy(
        src_ref=src,
        dst_ref=dst,
        send_sem=send_sem,
        recv_sem=recv_sem,
        device_id=device,
        device_id_type=MESH,
    )


def iota(shape, axis):
    return lax.broadcasted_iota(jnp.int32, shape, axis)


def gather_plan(nt):
    if nt == 16:
        return {0: (8, 4, -4, 1, -1, 2, -2), -4: (1, -1, 2), 4: (1, -1, -2), 8: (1, -1)}
    return {0: tuple(range(1, nt))}


def kernel(
    nt, ne, cap, units, half,
    og_in, rt_in, gc_in, cs_in, hs, dw,
    hg_out, sg_out, gg_out,
    og, rt, gc, cs, W, S, HS, QZ, SL, TM, TOKP, SRCP, QT, PMSG, PX, XP, QS, XQ, ACC, GB, HG,
    SPART, SPX, SSUM, SRECV, GM, GV, PV, PVR,
    lsem, wsem, ssem, zsem, qasem, qbsem, pxsem, prsem, psend, xqsem,
    gxsem, gzsem, spsem, srsem,
):
    d = lax.axis_index("dp")
    e = lax.axis_index("expert")
    t = lax.axis_index("tensor")
    side = math.isqrt(ne)
    ex, ey = lax.div(e, side), lax.rem(e, side)
    group = 8 * nt
    slots = ne * cap
    n_chunks = nt // 2
    chunk_w = 2 * LANES
    per_half = n_chunks // 2
    phalf = per_half * chunk_w
    qhalf = half - phalf
    part = qhalf // 2
    blocks = half // LANES
    reach = n_chunks // 2
    other = 1 - d

    def zpeer(k):
        return lax.rem(t + k + nt, nt)

    def xpeer(o):
        return lax.rem(ex + o // side, side) * side + lax.rem(ey + o % side, side)

    def at_z(k):
        return (d, e, zpeer(k))

    def at_x(o):
        return (d, xpeer(o), t)

    partner = (other, e, t)
    right, left = at_z(1), at_z(-1)

    def arrived(ref, sems):
        remote(ref, ref, sems.at[0], sems.at[1], partner).wait_recv()

    def left_here(ref, sems):
        remote(ref, ref, sems.at[0], sems.at[1], partner).wait_send()

    barrier = pltpu.get_barrier_semaphore()
    for k in sorted(range(1, nt), key=lambda k: -min(k, nt - k)):
        pl.semaphore_signal(barrier, inc=1, device_id=at_z(k), device_id_type=MESH)
    for o in range(ne - 1, 0, -1):
        pl.semaphore_signal(barrier, inc=1, device_id=at_x(o), device_id_type=MESH)
    pl.semaphore_signal(barrier, inc=1, device_id=partner, device_id_type=MESH)

    pairs = ((og_in, og), (cs_in, cs), (rt_in, rt), (gc_in, gc), (dw, W.at[d]), (hs, HS))
    loads = [pltpu.make_async_copy(a, b, lsem.at[i]) for i, (a, b) in enumerate(pairs)]
    for load in loads:
        load.start()
    for load in loads[:4]:
        load.wait()

    def two_rows(first, second, width):
        upper = og[:, first : first + width].astype(F32)
        lower = og[:, second : second + width].astype(F32)
        return jnp.concatenate([upper, lower], axis=0).astype(BF16)

    for i in (0, 1):
        QT[i, t] = two_rows(phalf + i * part, half + phalf + i * part, part)
    for j in range(n_chunks):
        start = (j // per_half) * half + (j % per_half) * chunk_w
        SRCP[j] = two_rows(start, start + LANES, LANES)
    TOKP[t] = SRCP[lax.rem(t, n_chunks)]
    S[d] = jnp.broadcast_to(cs[...].astype(F32), (8, half))

    pl.semaphore_wait(barrier, nt + ne - 1)

    plan = gather_plan(nt)
    via = [rel for rel in plan if rel]

    def send_tokens(i, rel, offsets):
        chunk = QT.at[i, zpeer(rel)]
        for k in offsets:
            seen = -k if k != 8 else 8
            recv = qasem.at[i, via.index(seen)] if rel == 0 and seen in via else qbsem.at[i, 1]
            remote(chunk, chunk, qbsem.at[i, 0], recv, at_z(k)).start()

    def tokens_from(i, rel):
        chunk = QT.at[i, zpeer(rel)]
        remote(chunk, chunk, qbsem.at[i, 0], qasem.at[i, via.index(rel)], partner).wait_recv()
        send_tokens(i, rel, plan[rel])

    for k in range(1, nt):
        source = SRCP.at[lax.rem(zpeer(k), n_chunks)]
        remote(source, TOKP.at[t], zsem.at[0], zsem.at[1], at_z(k)).start()
    send_tokens(0, 0, plan[0])
    send_tokens(1, 0, plan[0])
    remote(S.at[d], S.at[d], ssem.at[0], ssem.at[1], partner).start()
    remote(dw, W.at[d], wsem.at[0], wsem.at[1], partner).start()

    wide = 2 * group + group
    column = iota((group, wide), 1)
    token_of = jnp.where(
        column < 2 * group,
        lax.shift_right_logical(column, 4) * 8 + jnp.bitwise_and(column, 7),
        column - 2 * group,
    )
    row = iota((group, wide), 0)
    same = jnp.where(row == token_of, 1.0, 0.0).astype(BF16)
    earlier = jnp.where(row < token_of, 1.0, 0.0).astype(BF16)
    routes = jnp.dot(rt[...].astype(F32).astype(BF16), same, preferred_element_type=F32)
    codes = gc[...].astype(F32)
    name = [routes[k : k + 1] for k in (0, 1)]
    gate = [codes[k : k + 1] for k in (0, 1)]
    expert_row = iota((ne, wide), 0).astype(F32)
    names = [jnp.where(expert_row == name[k], 1.0, 0.0) for k in (0, 1)]
    both = (names[0] + names[1])[:, 2 * group :].astype(BF16)
    before = jnp.dot(both, earlier, preferred_element_type=F32)
    place = [jnp.sum(names[k] * before, axis=0, keepdims=True) for k in (0, 1)]
    slot = [name[k] * float(cap) + place[k] for k in (0, 1)]
    slot_row = iota((slots, wide), 0).astype(F32)
    picks = [jnp.where(slot_row == slot[k], 1.0, 0.0) for k in (0, 1)]
    pick = picks[0] + picks[1]
    in_half = jnp.bitwise_and(lax.shift_right_logical(iota((slots, 2 * group), 1), 3), 1)
    pick_q = [jnp.where(in_half == a, pick[:, : 2 * group], 0.0).astype(BF16) for a in (0, 1)]
    gate_pick = (
        picks[0][:, 2 * group :] * gate[0] + picks[1][:, 2 * group :] * gate[1]
    ).astype(BF16)
    gates = jnp.dot(gate_pick, jnp.ones((group, LANES), BF16), preferred_element_type=F32)
    PMSG[:, 2 * cap :, :] = (gates * (1.0 / 256.0)).astype(BF16).reshape(ne, cap, LANES)

    for load in loads[4:]:
        load.wait()

    def unit(hh, block):
        lanes = slice(block * 256, block * 256 + 256)
        scale = S[hh, 0:1, lanes]
        inverse = 1.0 / scale

        def rows(i, carry):
            at = pl.ds(pl.multiple_of(i * 128, 128), 128)
            u = W[hh, at, lanes].astype(F32) * inverse
            b = jnp.tanh(u)
            QZ[hh, at, lanes] = (scale * b).astype(BF16)
            SL[at, :] = (b - u * (1.0 - b * b)).astype(BF16)
            return carry

        lax.fori_loop(0, units // 128, rows, 0, unroll=True)
        TM[hh, :, lanes] = jnp.dot(HS[...], SL[...], preferred_element_type=F32)

    def partner_ready():
        arrived(S.at[other], ssem)
        arrived(W.at[other], wsem)

    def terms(x, hh, start):
        scaled = (x.astype(F32) * GB[...]).astype(BF16).astype(F32)
        return jnp.sum(scaled * TM[hh, :, pl.ds(start, LANES)], axis=0, keepdims=True)

    def chunk_p(j):
        hh = lax.div(j, per_half)
        b = lax.rem(j, per_half)
        start = pl.multiple_of(b * chunk_w, chunk_w)
        for i in (0, 1):
            x = XP[j, :, i * LANES : (i + 1) * LANES]
            SPART[hh, 2 * b + i] = terms(x, hh, pl.multiple_of(start + i * LANES, LANES))
        ACC[...] += lax.dot_general(
            XP[j],
            QZ[hh, :, pl.ds(start, chunk_w)],
            (((1,), (1,)), ((), ())),
            preferred_element_type=F32,
        )

    def parts_q(i):
        for a in (0, 1):
            for c in range(part // LANES):
                at = i * part + c * LANES
                x = XQ[i, :, :, a * part + c * LANES : a * part + (c + 1) * LANES]
                SPART[a, (phalf + at) // LANES] = terms(x.reshape(slots, LANES), a, phalf + at)

    def dot_q(i):
        for a in (0, 1):
            ACC[...] += lax.dot_general(
                XQ[i, :, :, a * part : (a + 1) * part].reshape(slots, part),
                QZ[a, :, phalf + i * part : phalf + (i + 1) * part],
                (((1,), (1,)), ((), ())),
                preferred_element_type=F32,
            )

    pb, qb = phalf // 256, qhalf // 256
    work = [functools.partial(unit, d, b) for b in range(pb)]
    work += [partner_ready]
    work += [functools.partial(unit, other, b) for b in range(pb)]
    work += [functools.partial(unit, h, pb + b) for b in range(qb) for h in (d, other)]
    chunks = [functools.partial(chunk_p, lax.rem(t, n_chunks))]
    for k in range(1, reach):
        for rel in (-k, k):
            chunks += [functools.partial(chunk_p, lax.rem(zpeer(rel), n_chunks))]
    chunks += [functools.partial(chunk_p, lax.rem(zpeer(reach), n_chunks))]

    def do(jobs, n):
        for _ in range(n):
            if jobs:
                jobs.pop(0)()


    do(work, pb)
    for rel in via[:2]:
        tokens_from(0, rel)

    arrived(TOKP.at[pl.ds(0, nt - 1)], zsem)
    tokens = TOKP[...].reshape(2 * group, LANES)
    for a in (0, 1):
        routed = jnp.dot(pick_q[a], tokens, preferred_element_type=F32).astype(BF16)
        PMSG[:, a * cap : (a + 1) * cap, :] = routed.reshape(ne, cap, LANES)
    for o in range(1, ne):
        remote(PMSG.at[xpeer(o)], PX.at[e], pxsem.at[0], pxsem.at[1], at_x(o)).start()
    PX[e] = PMSG[e]

    for rel in via[2:]:
        tokens_from(0, rel)
    for rel in via:
        tokens_from(1, rel)
    do(work, 1 + pb)

    n_direct = nt - 1 - len(via)

    def route_q(i):
        arrived(QT.at[i, pl.ds(0, n_direct)], qbsem.at[i])
        gathered = QT[i].reshape(2 * group, part)
        step = min(256, part)
        for a in (0, 1):
            for c in range(0, part, step):
                QS[i, :, :, a * part + c : a * part + c + step] = (
                    jnp.dot(pick_q[a], gathered[:, c : c + step], preferred_element_type=F32)
                    .astype(BF16)
                    .reshape(ne, cap, step)
                )
        for o in range(1, ne):
            remote(QS.at[i, xpeer(o)], XQ.at[i, e], xqsem.at[i, 0], xqsem.at[i, 1], at_x(o)).start()
        XQ[i, e] = QS[i, e]

    pieces = 8
    prow = slots // pieces

    def piece(j, i):
        return XP.at[j, pl.ds(i * prow, prow)]

    def pass_on(way, rel, k, i):
        if k == reach and (i < pieces // 2) != (way == 0):
            return
        ref = piece(lax.rem(zpeer(rel), n_chunks), i)
        remote(ref, ref, psend.at[way], prsem.at[way, k, i], (right, left)[way]).start()

    def ring_p(k):
        for i in range(pieces):
            for way in (0, 1):
                if k == reach and (i < pieces // 2) != (way == 0):
                    continue
                rel = -k if way == 0 else k
                ref = piece(lax.rem(zpeer(rel), n_chunks), i)
                remote(ref, ref, psend.at[way], prsem.at[way, k, i], partner).wait_recv()
                if k < reach:
                    pass_on(way, rel, k + 1, i)

    arrived(PX.at[pl.ds(0, ne - 1)], pxsem)
    mine_p = lax.rem(t, n_chunks)
    for a in (0, 1):
        XP[mine_p, :, a * LANES : (a + 1) * LANES] = PX[:, a * cap : (a + 1) * cap, :].reshape(slots, LANES)
    for i in range(pieces):
        for way in (0, 1):
            pass_on(way, 0, 1, i)
    route_q(0)
    GB[...] = PX[:, 2 * cap :, :].reshape(slots, LANES).astype(F32)
    ACC[...] = jnp.zeros_like(ACC)
    route_q(1)

    do(work, qb)
    for k in range(1, reach):
        ring_p(k)
        do(work, len(work))
        do(chunks, 3 if k == 1 else 2)
    do(work, len(work))
    arrived(XQ.at[0, pl.ds(0, ne - 1)], xqsem.at[0])
    parts_q(0)
    dot_q(0)
    ring_p(reach)
    do(chunks, len(chunks))
    arrived(XQ.at[1, pl.ds(0, ne - 1)], xqsem.at[1])
    dot_q(1)

    weighed = ACC[:, 0:LANES] * HS[:, 0:LANES].astype(F32)
    for c in range(LANES, units, LANES):
        weighed += ACC[:, c : c + LANES] * HS[:, c : c + LANES].astype(F32)
    weighed = jnp.sum(weighed, axis=1, keepdims=True)
    at_place = jnp.bitwise_and(iota((slots, LANES), 0), cap - 1) == iota((slots, LANES), 1)
    GM[...] = jnp.sum(
        jnp.where(at_place, weighed, 0.0).reshape(ne, cap, LANES), axis=1, keepdims=True
    )
    for o in range(1, ne):
        remote(GM.at[xpeer(o)], GV.at[e], gxsem.at[0], gxsem.at[1], at_x(o)).start()
    GV[e] = GM[e]

    parts_q(1)
    remote(SPART.at[other], SPX, spsem.at[0], spsem.at[1], partner).start()
    arrived(SPX, spsem)
    SSUM[...] = SPART[d] + SPX[...]
    for k in range(1, nt):
        remote(SSUM, SRECV.at[t], srsem.at[0], srsem.at[1], at_z(k)).start()
    SRECV[t] = SSUM[...]

    for c in range(0, units, LANES):
        HG[:, c : c + LANES] = (ACC[:, c : c + LANES] * GB[...]).astype(BF16)
    save = pltpu.make_async_copy(HG, hg_out, lsem.at[0])
    save.start()

    arrived(GV.at[pl.ds(0, ne - 1)], gxsem)
    values = jnp.concatenate([GV[i] for i in range(ne)], axis=0)
    place_row = iota((LANES, group), 0).astype(F32)
    pair_rows = []
    for k in (0, 1):
        chosen = jnp.where(place_row == place[k][:, 2 * group :], 1.0, 0.0)
        spread = jnp.dot(values, chosen, precision=lax.Precision.HIGHEST, preferred_element_type=F32)
        pair_rows.append(jnp.sum(spread * names[k][:, 2 * group :], axis=0, keepdims=True))
    PV[...] = jnp.concatenate(pair_rows, axis=0)
    for k in range(1, nt):
        remote(PV, PVR.at[t], gzsem.at[0], gzsem.at[1], at_z(k)).start()
    PVR[t] = PV[...]

    arrived(SRECV.at[pl.ds(0, nt - 1)], srsem)
    total = SRECV[0]
    for i in range(1, nt):
        total += SRECV[i]
    for i in range(blocks):
        sg_out[:, i * LANES : (i + 1) * LANES] = total[i]

    arrived(PVR.at[pl.ds(0, nt - 1)], gzsem)
    total = PVR[0]
    for i in range(1, nt):
        total += PVR[i]
    mine = jnp.where(iota((group, 8), 0) == t * 8 + iota((group, 8), 1), 1.0, 0.0)
    gg_out[...] = jnp.dot(total, mine, precision=lax.Precision.HIGHEST, preferred_element_type=F32)

    left_here(TOKP.at[pl.ds(0, nt - 1)], zsem)
    left_here(S.at[d], ssem)
    left_here(dw, wsem)
    left_here(PMSG.at[pl.ds(0, ne - 1)], pxsem)
    for i in (0, 1):
        left_here(QT.at[i, pl.ds(0, nt - 1)], qbsem.at[i])
        left_here(QS.at[i, pl.ds(0, ne - 1)], xqsem.at[i])
    for way in (0, 1):
        ref = XP.at[pl.ds(0, 2 * reach - 1), pl.ds(0, slots // 2)]
        remote(ref, ref, psend.at[way], prsem.at[way, 1, 0], partner).wait_send()
    left_here(GM.at[pl.ds(0, ne - 1)], gxsem)
    left_here(PVR.at[pl.ds(0, nt - 1)], gzsem)
    left_here(SPX, spsem)
    left_here(SRECV.at[pl.ds(0, nt - 1)], srsem)
    save.wait()


def write_kernel(hg, sg, gg, hg_out, sg_out, gg_out):
    hg_out[...] = hg[...]
    sg_out[...] = sg[...]
    gg_out[...] = gg[...]


def on_device(nt, ne, out_grad, routing, gate_codes, hidden_saved, down_weight, channel_scale):
    cap = hidden_saved.shape[3]
    units = hidden_saved.shape[4]
    half = down_weight.shape[2]
    group = routing.shape[0]
    slots = ne * cap
    n_chunks = nt // 2
    qhalf = half - n_chunks * LANES
    blocks = half // LANES
    vmem = pl.BlockSpec(memory_space=pltpu.VMEM)
    anywhere = pl.BlockSpec(memory_space=pl.ANY)
    dma = pltpu.SemaphoreType.DMA
    results = (
        jax.ShapeDtypeStruct((slots, units), BF16),
        jax.ShapeDtypeStruct((1, half), F32),
        jax.ShapeDtypeStruct((2, 8), F32),
    )
    parts = pl.pallas_call(
        functools.partial(kernel, nt, ne, cap, units, half),
        out_shape=results,
        in_specs=[anywhere] * 6,
        out_specs=(anywhere, vmem, vmem),
        scratch_shapes=[
            pltpu.VMEM(out_grad.shape, BF16),
            pltpu.VMEM((2, group), jnp.int32),
            pltpu.VMEM((2, group), jnp.int32),
            pltpu.VMEM((1, half), BF16),
            pltpu.VMEM((2, units, half), BF16),
            pltpu.VMEM((2, 8, half), F32),
            pltpu.VMEM((slots, units), BF16),
            pltpu.VMEM((2, units, half), BF16),
            pltpu.VMEM((units, 256), BF16),
            pltpu.VMEM((2, slots, half), F32),
            pltpu.VMEM((nt, 16, LANES), BF16),
            pltpu.VMEM((n_chunks, 16, LANES), BF16),
            pltpu.VMEM((2, nt, 16, qhalf // 2), BF16),
            pltpu.VMEM((ne, 3 * cap, LANES), BF16),
            pltpu.VMEM((ne, 3 * cap, LANES), BF16),
            pltpu.VMEM((n_chunks, slots, 2 * LANES), BF16),
            pltpu.VMEM((2, ne, cap, qhalf), BF16),
            pltpu.VMEM((2, ne, cap, qhalf), BF16),
            pltpu.VMEM((slots, units), F32),
            pltpu.VMEM((slots, LANES), F32),
            pltpu.VMEM((slots, units), BF16),
            pltpu.VMEM((2, blocks, 1, LANES), F32),
            pltpu.VMEM((blocks, 1, LANES), F32),
            pltpu.VMEM((blocks, 1, LANES), F32),
            pltpu.VMEM((nt, blocks, 1, LANES), F32),
            pltpu.VMEM((ne, 1, LANES), F32),
            pltpu.VMEM((ne, 1, LANES), F32),
            pltpu.VMEM((2, group), F32),
            pltpu.VMEM((nt, 2, group), F32),
            dma((6,)),
            dma((2,)),
            dma((2,)),
            dma((2,)),
            dma((2, 3)),
            dma((2, 2)),
            dma((2,)),
            dma((2, n_chunks // 2 + 1, 8)),
            dma((2,)),
            dma((2, 2)),
            dma((2,)),
            dma((2,)),
            dma((2,)),
            dma((2,)),
        ],
        compiler_params=pltpu.CompilerParams(
            collective_id=0, has_side_effects=True, vmem_limit_bytes=60 * 1024 * 1024
        ),
    )(
        out_grad,
        routing.T,
        gate_codes.T,
        channel_scale,
        hidden_saved.reshape(slots, units),
        down_weight.reshape(units, half),
    )
    hidden_grad, scale_grad, gate_grad = pl.pallas_call(
        write_kernel,
        out_shape=results,
        in_specs=[vmem] * 3,
        out_specs=(vmem,) * 3,
    )(*parts)
    return hidden_grad.reshape(hidden_saved.shape), scale_grad, gate_grad.T


def solution(mesh):
    in_specs = (
        P(("dp", "expert", "tensor"), None),
        P(("dp", "expert"), None),
        P(("dp", "expert"), None),
        P("dp", "expert", None, None, "tensor"),
        P("expert", "tensor", "dp"),
        P("expert", "dp"),
    )
    out_specs = (
        P("dp", "expert", None, None, "tensor"),
        P("expert", "dp"),
        P(("dp", "expert", "tensor"), None),
    )
    return jax.shard_map(
        functools.partial(on_device, mesh.shape["tensor"], mesh.shape["expert"]),
        mesh=mesh,
        in_specs=in_specs,
        out_specs=out_specs,
        check_vma=False,
    )
```

```python
import functools
import math

import jax
import jax.numpy as jnp
from jax import lax
from jax.experimental import pallas as pl
from jax.experimental.pallas import tpu as pltpu
from jax.sharding import PartitionSpec as P

MESH = pl.DeviceIdType.MESH
F32 = jnp.float32
BF16 = jnp.bfloat16
LANES = 128


def remote(src, dst, send_sem, recv_sem, device):
    return pltpu.make_async_remote_copy(
        src_ref=src,
        dst_ref=dst,
        send_sem=send_sem,
        recv_sem=recv_sem,
        device_id=device,
        device_id_type=MESH,
    )


def iota(shape, axis):
    return lax.broadcasted_iota(jnp.int32, shape, axis)


def three_parts(x):
    first = x.astype(BF16)
    rest = x - first.astype(F32)
    second = rest.astype(BF16)
    third = (rest - second.astype(F32)).astype(BF16)
    return jnp.concatenate([first, second, third], axis=0)


def part_widths(qhalf):
    if qhalf == 8 * LANES:
        return (2 * LANES, 3 * LANES, 3 * LANES)
    return (LANES,) * (qhalf // LANES)


def gather_plan(nt, i):
    if nt == 16 and i > 0:
        return {0: (8, 4, -4, 1, -1, 2, -2), -4: (1, -1, 2), 4: (1, -1, -2), 8: (1, -1)}
    return {0: tuple(sorted(range(1, nt), key=lambda k: -min(k, nt - k)))}


def kernel(
    nt, ne, cap, units, half,
    og_in, rt_in, gc_in, cs_in, hs, dw,
    hg_out, sg_out, gg_out,
    og, rt, gc, cs, W, S, HS, QZ, SL, TM, TOKP, SRCP, QT, PMSG, PX, XP, QS, XQ, ACC, GB, HG,
    SPART, SPX, SSUM, SRECV, GM, GV, PV, PVR, CH, NM,
    lsem, wsem, ssem, zsem, qasem, qbsem, pxsem, prsem, psend, xqsem,
    gxsem, gzsem, spsem, srsem,
):
    d = lax.axis_index("dp")
    e = lax.axis_index("expert")
    t = lax.axis_index("tensor")
    side = math.isqrt(ne)
    ex, ey = lax.div(e, side), lax.rem(e, side)
    group = 8 * nt
    slots = ne * cap
    n_chunks = nt // 2
    chunk_w = 2 * LANES
    per_half = n_chunks // 2
    phalf = per_half * chunk_w
    qhalf = half - phalf
    widths = part_widths(qhalf)
    offsets = [phalf + sum(widths[:i]) for i in range(len(widths))]
    last = len(widths) - 1
    blocks = half // LANES
    reach = n_chunks // 2
    other = 1 - d

    def zpeer(k):
        return lax.rem(t + k + nt, nt)

    def xpeer(o):
        return lax.rem(ex + o // side, side) * side + lax.rem(ey + o % side, side)

    def at_z(k):
        return (d, e, zpeer(k))

    def at_x(o):
        return (d, xpeer(o), t)

    partner = (other, e, t)
    right, left = at_z(1), at_z(-1)

    def arrived(ref, sems):
        remote(ref, ref, sems.at[0], sems.at[1], partner).wait_recv()

    def left_here(ref, sems):
        remote(ref, ref, sems.at[0], sems.at[1], partner).wait_send()

    barrier = pltpu.get_barrier_semaphore()
    for k in sorted(range(1, nt), key=lambda k: -min(k, nt - k)):
        pl.semaphore_signal(barrier, inc=1, device_id=at_z(k), device_id_type=MESH)
    for o in range(ne - 1, 0, -1):
        pl.semaphore_signal(barrier, inc=1, device_id=at_x(o), device_id_type=MESH)
    pl.semaphore_signal(barrier, inc=1, device_id=partner, device_id_type=MESH)

    pairs = ((og_in, og), (cs_in, cs), (rt_in, rt), (gc_in, gc), (dw, W.at[d]), (hs, HS))
    loads = [pltpu.make_async_copy(a, b, lsem.at[i]) for i, (a, b) in enumerate(pairs)]
    for load in loads:
        load.start()
    for load in loads[:4]:
        load.wait()

    def two_rows(first, second, width):
        upper = og[:, first : first + width].astype(F32)
        lower = og[:, second : second + width].astype(F32)
        return jnp.concatenate([upper, lower], axis=0).astype(BF16)

    for i, width in enumerate(widths):
        QT[i][t] = two_rows(offsets[i], half + offsets[i], width)
    for j in range(n_chunks):
        start = (j // per_half) * half + (j % per_half) * chunk_w
        SRCP[j] = two_rows(start, start + LANES, LANES)
    TOKP[t] = SRCP[lax.rem(t, n_chunks)]
    S[d] = jnp.broadcast_to(cs[...].astype(F32), (8, half))

    pl.semaphore_wait(barrier, nt + ne - 1)

    plans = [gather_plan(nt, i) for i in range(len(widths))]
    vias = [[rel for rel in plan if rel] for plan in plans]

    def send_tokens(i, rel):
        chunk = QT[i].at[zpeer(rel)]
        for k in plans[i][rel]:
            seen = -k if k != 8 else 8
            known = rel == 0 and seen in vias[i]
            recv = qasem.at[i, vias[i].index(seen)] if known else qbsem.at[i, 1]
            remote(chunk, chunk, qbsem.at[i, 0], recv, at_z(k)).start()

    def tokens_from(i, rels):
        for rel in rels:
            chunk = QT[i].at[zpeer(rel)]
            sem = qasem.at[i, vias[i].index(rel)]
            remote(chunk, chunk, qbsem.at[i, 0], sem, partner).wait_recv()
            send_tokens(i, rel)

    for k in range(1, nt):
        source = SRCP.at[lax.rem(zpeer(k), n_chunks)]
        remote(source, TOKP.at[t], zsem.at[0], zsem.at[1], at_z(k)).start()
    for i in range(len(widths)):
        send_tokens(i, 0)
    remote(S.at[d], S.at[d], ssem.at[0], ssem.at[1], partner).start()
    remote(dw, W.at[d], wsem.at[0], wsem.at[1], partner).start()

    wide = 2 * group + group
    column = iota((group, wide), 1)
    token_of = jnp.where(
        column < 2 * group,
        lax.shift_right_logical(column, 4) * 8 + jnp.bitwise_and(column, 7),
        column - 2 * group,
    )
    row = iota((group, wide), 0)
    same = jnp.where(row == token_of, 1.0, 0.0).astype(BF16)
    earlier = jnp.where(row < token_of, 1.0, 0.0).astype(BF16)
    routes = jnp.dot(rt[...].astype(F32).astype(BF16), same, preferred_element_type=F32)
    codes = gc[...].astype(F32)
    name = [routes[k : k + 1] for k in (0, 1)]
    gate = [codes[k : k + 1] for k in (0, 1)]
    expert_row = iota((ne, wide), 0).astype(F32)
    names = [jnp.where(expert_row == name[k], 1.0, 0.0) for k in (0, 1)]
    both = (names[0] + names[1])[:, 2 * group :].astype(BF16)
    before = jnp.dot(both, earlier, preferred_element_type=F32)
    place = [jnp.sum(names[k] * before, axis=0, keepdims=True) for k in (0, 1)]
    slot = [name[k] * float(cap) + place[k] for k in (0, 1)]
    slot_row = iota((slots, wide), 0).astype(F32)
    picks = [jnp.where(slot_row == slot[k], 1.0, 0.0) for k in (0, 1)]
    pick = picks[0] + picks[1]
    in_half = jnp.bitwise_and(lax.shift_right_logical(iota((slots, 2 * group), 1), 3), 1)
    pick_q = [jnp.where(in_half == a, pick[:, : 2 * group], 0.0).astype(BF16) for a in (0, 1)]
    gate_pick = (
        picks[0][:, 2 * group :] * gate[0] + picks[1][:, 2 * group :] * gate[1]
    ).astype(BF16)
    gates = jnp.dot(gate_pick, jnp.ones((group, LANES), BF16), preferred_element_type=F32)
    PMSG[:, 2 * cap :, :] = (gates * (1.0 / 256.0)).astype(BF16).reshape(ne, cap, LANES)

    place_row = iota((LANES, group), 0).astype(F32)
    for k in (0, 1):
        at = slice(k * group, (k + 1) * group)
        CH[:, at] = jnp.where(place_row == place[k][:, 2 * group :], 1.0, 0.0).astype(BF16)
        NM[:, at] = names[k][:, 2 * group :]
    for load in loads[4:]:
        load.wait()

    def unit(hh, block):
        lanes = slice(block * 256, block * 256 + 256)
        scale = S[hh, 0:1, lanes]
        inverse = 1.0 / scale

        def rows(i, carry):
            at = pl.ds(pl.multiple_of(i * 128, 128), 128)
            u = W[hh, at, lanes].astype(F32) * inverse
            b = jnp.tanh(u)
            QZ[hh, at, lanes] = (scale * b).astype(BF16)
            SL[at, :] = (b - u * (1.0 - b * b)).astype(BF16)
            return carry

        lax.fori_loop(0, units // 128, rows, 0, unroll=True)
        TM[hh, :, lanes] = jnp.dot(HS[...], SL[...], preferred_element_type=F32)

    def partner_ready():
        arrived(S.at[other], ssem)
        arrived(W.at[other], wsem)

    def terms(x, hh, start):
        scaled = (x.astype(F32) * GB[...]).astype(BF16).astype(F32)
        return jnp.sum(scaled * TM[hh, :, pl.ds(start, LANES)], axis=0, keepdims=True)

    def chunk_p(j):
        hh = lax.div(j, per_half)
        b = lax.rem(j, per_half)
        start = pl.multiple_of(b * chunk_w, chunk_w)
        for i in (0, 1):
            x = XP[j, :, i * LANES : (i + 1) * LANES]
            SPART[hh, 2 * b + i] = terms(x, hh, pl.multiple_of(start + i * LANES, LANES))
        ACC[...] += lax.dot_general(
            XP[j],
            QZ[hh, :, pl.ds(start, chunk_w)],
            (((1,), (1,)), ((), ())),
            preferred_element_type=F32,
        )

    def parts_q(i):
        width = widths[i]
        for a in (0, 1):
            for c in range(width // LANES):
                at = offsets[i] + c * LANES
                x = XQ[i][:, :, a * width + c * LANES : a * width + (c + 1) * LANES]
                SPART[a, at // LANES] = terms(x.reshape(slots, LANES), a, at)

    def dot_q(i):
        lanes = slice(offsets[i], offsets[i] + widths[i])
        ACC[...] += lax.dot_general(
            XQ[i][...].reshape(slots, 2 * widths[i]),
            jnp.concatenate([QZ[0, :, lanes], QZ[1, :, lanes]], axis=1),
            (((1,), (1,)), ((), ())),
            preferred_element_type=F32,
        )

    def arrived_q(i):
        arrived(XQ[i].at[pl.ds(0, ne - 1)], xqsem.at[i])

    pb, qb = phalf // 256, qhalf // 256
    work = [functools.partial(unit, d, b) for b in range(pb)]
    work += [partner_ready]
    work += [functools.partial(unit, other, b) for b in range(pb)]
    work += [functools.partial(unit, h, pb + b) for b in range(qb) for h in (d, other)]
    chunks = [functools.partial(chunk_p, lax.rem(t, n_chunks))]
    for k in range(1, reach):
        for rel in (-k, k):
            chunks += [functools.partial(chunk_p, lax.rem(zpeer(rel), n_chunks))]
    chunks += [functools.partial(chunk_p, lax.rem(zpeer(reach), n_chunks))]

    def do(jobs, n):
        for _ in range(n):
            if jobs:
                jobs.pop(0)()


    do(work, pb)

    arrived(TOKP.at[pl.ds(0, nt - 1)], zsem)
    tokens = TOKP[...].reshape(2 * group, LANES)
    for a in (0, 1):
        routed = jnp.dot(pick_q[a], tokens, preferred_element_type=F32).astype(BF16)
        PMSG[:, a * cap : (a + 1) * cap, :] = routed.reshape(ne, cap, LANES)
    for o in range(1, ne):
        remote(PMSG.at[xpeer(o)], PX.at[e], pxsem.at[0], pxsem.at[1], at_x(o)).start()
    PX[e] = PMSG[e]

    def route_q(i):
        width = widths[i]
        arrived(QT[i].at[pl.ds(0, nt - 1 - len(vias[i]))], qbsem.at[i])
        gathered = QT[i][...].reshape(2 * group, width)
        for a in (0, 1):
            QS[i][:, :, a * width : (a + 1) * width] = (
                jnp.dot(pick_q[a], gathered, preferred_element_type=F32)
                .astype(BF16)
                .reshape(ne, cap, width)
            )
        for o in range(1, ne):
            source, target = QS[i].at[xpeer(o)], XQ[i].at[e]
            remote(source, target, xqsem.at[i, 0], xqsem.at[i, 1], at_x(o)).start()
        XQ[i][e] = QS[i][e]

    for i in range(1, len(widths)):
        tokens_from(i, vias[i][:2])
        if i == 1:
            route_q(0)
    for i in range(1, len(widths)):
        tokens_from(i, vias[i][2:])
    do(work, 1 + pb)

    pieces = 8
    prow = slots // pieces

    def piece(j, i):
        return XP.at[j, pl.ds(i * prow, prow)]

    def pass_on(way, rel, k, i):
        if k == reach and (i < pieces // 2) != (way == 0):
            return
        ref = piece(lax.rem(zpeer(rel), n_chunks), i)
        remote(ref, ref, psend.at[way], prsem.at[way, k, i], (right, left)[way]).start()

    def ring_p(k):
        for i in range(pieces):
            for way in (0, 1):
                if k == reach and (i < pieces // 2) != (way == 0):
                    continue
                rel = -k if way == 0 else k
                ref = piece(lax.rem(zpeer(rel), n_chunks), i)
                remote(ref, ref, psend.at[way], prsem.at[way, k, i], partner).wait_recv()
                if k < reach:
                    pass_on(way, rel, k + 1, i)

    arrived(PX.at[pl.ds(0, ne - 1)], pxsem)
    mine_p = lax.rem(t, n_chunks)
    for a in (0, 1):
        XP[mine_p, :, a * LANES : (a + 1) * LANES] = PX[:, a * cap : (a + 1) * cap, :].reshape(slots, LANES)
    for i in range(pieces):
        for way in (0, 1):
            pass_on(way, 0, 1, i)
    route_q(1)
    GB[...] = PX[:, 2 * cap :, :].reshape(slots, LANES).astype(F32)
    ACC[...] = jnp.zeros_like(ACC)
    for i in range(2, len(widths)):
        route_q(i)

    do(work, qb)
    for k in range(1, reach):
        ring_p(k)
        do(work, len(work))
        do(chunks, 3 if k == 1 else 2)
    do(work, len(work))
    for i in range(last):
        arrived_q(i)
        parts_q(i)
        dot_q(i)
    ring_p(reach)
    do(chunks, len(chunks))
    arrived_q(last)
    dot_q(last)

    weighed = ACC[:, 0:LANES] * HS[:, 0:LANES].astype(F32)
    for c in range(LANES, units, LANES):
        weighed += ACC[:, c : c + LANES] * HS[:, c : c + LANES].astype(F32)
    weighed = jnp.sum(weighed, axis=1, keepdims=True)
    at_place = jnp.bitwise_and(iota((slots, LANES), 0), cap - 1) == iota((slots, LANES), 1)
    GM[...] = jnp.sum(
        jnp.where(at_place, weighed, 0.0).reshape(ne, cap, LANES), axis=1, keepdims=True
    )
    for o in range(1, ne):
        remote(GM.at[xpeer(o)], GV.at[e], gxsem.at[0], gxsem.at[1], at_x(o)).start()
    GV[e] = GM[e]

    parts_q(last)
    remote(SPART.at[other], SPX, spsem.at[0], spsem.at[1], partner).start()
    arrived(SPX, spsem)
    SSUM[...] = SPART[d] + SPX[...]
    for k in range(1, nt):
        remote(SSUM, SRECV.at[t], srsem.at[0], srsem.at[1], at_z(k)).start()
    SRECV[t] = SSUM[...]

    for c in range(0, units, LANES):
        HG[:, c : c + LANES] = (ACC[:, c : c + LANES] * GB[...]).astype(BF16)
    save = pltpu.make_async_copy(HG, hg_out, lsem.at[0])
    save.start()

    arrived(GV.at[pl.ds(0, ne - 1)], gxsem)
    values = jnp.concatenate([GV[i] for i in range(ne)], axis=0)
    spread = jnp.dot(three_parts(values), CH[...], preferred_element_type=F32)
    spread = (spread[:ne] + spread[ne : 2 * ne] + spread[2 * ne :]) * NM[...]
    pair_row = jnp.sum(spread, axis=0, keepdims=True)
    pair_rows = [pair_row[:, :group], pair_row[:, group:]]
    PV[...] = jnp.concatenate(pair_rows, axis=0)
    for k in range(1, nt):
        remote(PV, PVR.at[t], gzsem.at[0], gzsem.at[1], at_z(k)).start()
    PVR[t] = PV[...]

    arrived(SRECV.at[pl.ds(0, nt - 1)], srsem)
    total = SRECV[0]
    for i in range(1, nt):
        total += SRECV[i]
    for i in range(blocks):
        sg_out[:, i * LANES : (i + 1) * LANES] = total[i]

    arrived(PVR.at[pl.ds(0, nt - 1)], gzsem)
    total = PVR[0]
    for i in range(1, nt):
        total += PVR[i]
    mine = jnp.where(iota((group, 8), 0) == t * 8 + iota((group, 8), 1), 1.0, 0.0).astype(BF16)
    picked = jnp.dot(three_parts(total), mine, preferred_element_type=F32)
    gg_out[...] = picked[0:2] + picked[2:4] + picked[4:6]

    left_here(TOKP.at[pl.ds(0, nt - 1)], zsem)
    left_here(S.at[d], ssem)
    left_here(dw, wsem)
    left_here(PMSG.at[pl.ds(0, ne - 1)], pxsem)
    for i in range(len(widths)):
        left_here(QT[i].at[pl.ds(0, nt - 1)], qbsem.at[i])
        left_here(QS[i].at[pl.ds(0, ne - 1)], xqsem.at[i])
    for way in (0, 1):
        ref = XP.at[pl.ds(0, 2 * reach - 1), pl.ds(0, slots // 2)]
        remote(ref, ref, psend.at[way], prsem.at[way, 1, 0], partner).wait_send()
    left_here(GM.at[pl.ds(0, ne - 1)], gxsem)
    left_here(PVR.at[pl.ds(0, nt - 1)], gzsem)
    left_here(SPX, spsem)
    left_here(SRECV.at[pl.ds(0, nt - 1)], srsem)
    save.wait()


def write_kernel(hg, sg, gg, hg_out, sg_out, gg_out):
    hg_out[...] = hg[...]
    sg_out[...] = sg[...]
    gg_out[...] = gg[...]


def on_device(nt, ne, out_grad, routing, gate_codes, hidden_saved, down_weight, channel_scale):
    cap = hidden_saved.shape[3]
    units = hidden_saved.shape[4]
    half = down_weight.shape[2]
    group = routing.shape[0]
    slots = ne * cap
    n_chunks = nt // 2
    widths = part_widths(half - n_chunks * LANES)
    blocks = half // LANES
    vmem = pl.BlockSpec(memory_space=pltpu.VMEM)
    anywhere = pl.BlockSpec(memory_space=pl.ANY)
    dma = pltpu.SemaphoreType.DMA
    results = (
        jax.ShapeDtypeStruct((slots, units), BF16),
        jax.ShapeDtypeStruct((1, half), F32),
        jax.ShapeDtypeStruct((2, 8), F32),
    )
    parts = pl.pallas_call(
        functools.partial(kernel, nt, ne, cap, units, half),
        out_shape=results,
        in_specs=[anywhere] * 6,
        out_specs=(anywhere, vmem, vmem),
        scratch_shapes=[
            pltpu.VMEM(out_grad.shape, BF16),
            pltpu.VMEM((2, group), jnp.int32),
            pltpu.VMEM((2, group), jnp.int32),
            pltpu.VMEM((1, half), BF16),
            pltpu.VMEM((2, units, half), BF16),
            pltpu.VMEM((2, 8, half), F32),
            pltpu.VMEM((slots, units), BF16),
            pltpu.VMEM((2, units, half), BF16),
            pltpu.VMEM((units, 256), BF16),
            pltpu.VMEM((2, slots, half), F32),
            pltpu.VMEM((nt, 16, LANES), BF16),
            pltpu.VMEM((n_chunks, 16, LANES), BF16),
            [pltpu.VMEM((nt, 16, w), BF16) for w in widths],
            pltpu.VMEM((ne, 3 * cap, LANES), BF16),
            pltpu.VMEM((ne, 3 * cap, LANES), BF16),
            pltpu.VMEM((n_chunks, slots, 2 * LANES), BF16),
            [pltpu.VMEM((ne, cap, 2 * w), BF16) for w in widths],
            [pltpu.VMEM((ne, cap, 2 * w), BF16) for w in widths],
            pltpu.VMEM((slots, units), F32),
            pltpu.VMEM((slots, LANES), F32),
            pltpu.VMEM((slots, units), BF16),
            pltpu.VMEM((2, blocks, 1, LANES), F32),
            pltpu.VMEM((blocks, 1, LANES), F32),
            pltpu.VMEM((blocks, 1, LANES), F32),
            pltpu.VMEM((nt, blocks, 1, LANES), F32),
            pltpu.VMEM((ne, 1, LANES), F32),
            pltpu.VMEM((ne, 1, LANES), F32),
            pltpu.VMEM((2, group), F32),
            pltpu.VMEM((nt, 2, group), F32),
            pltpu.VMEM((LANES, 2 * group), BF16),
            pltpu.VMEM((ne, 2 * group), F32),
            dma((6,)),
            dma((2,)),
            dma((2,)),
            dma((2,)),
            dma((len(widths), 3)),
            dma((len(widths), 2)),
            dma((2,)),
            dma((2, n_chunks // 2 + 1, 8)),
            dma((2,)),
            dma((len(widths), 2)),
            dma((2,)),
            dma((2,)),
            dma((2,)),
            dma((2,)),
        ],
        compiler_params=pltpu.CompilerParams(
            collective_id=0, has_side_effects=True, vmem_limit_bytes=60 * 1024 * 1024
        ),
    )(
        out_grad,
        routing.T,
        gate_codes.T,
        channel_scale,
        hidden_saved.reshape(slots, units),
        down_weight.reshape(units, half),
    )
    hidden_grad, scale_grad, gate_grad = pl.pallas_call(
        write_kernel,
        out_shape=results,
        in_specs=[vmem] * 3,
        out_specs=(vmem,) * 3,
    )(*parts)
    return hidden_grad.reshape(hidden_saved.shape), scale_grad, gate_grad.T


def solution(mesh):
    in_specs = (
        P(("dp", "expert", "tensor"), None),
        P(("dp", "expert"), None),
        P(("dp", "expert"), None),
        P("dp", "expert", None, None, "tensor"),
        P("expert", "tensor", "dp"),
        P("expert", "dp"),
    )
    out_specs = (
        P("dp", "expert", None, None, "tensor"),
        P("expert", "dp"),
        P(("dp", "expert", "tensor"), None),
    )
    return jax.shard_map(
        functools.partial(on_device, mesh.shape["tensor"], mesh.shape["expert"]),
        mesh=mesh,
        in_specs=in_specs,
        out_specs=out_specs,
        check_vma=False,
    )
```

```python
import functools
import math

import jax
import jax.numpy as jnp
from jax import lax
from jax.experimental import pallas as pl
from jax.experimental.pallas import tpu as pltpu
from jax.sharding import PartitionSpec as P

MESH = pl.DeviceIdType.MESH
F32 = jnp.float32
BF16 = jnp.bfloat16
LANES = 128


def remote(src, dst, send_sem, recv_sem, device):
    return pltpu.make_async_remote_copy(
        src_ref=src,
        dst_ref=dst,
        send_sem=send_sem,
        recv_sem=recv_sem,
        device_id=device,
        device_id_type=MESH,
    )


def iota(shape, axis):
    return lax.broadcasted_iota(jnp.int32, shape, axis)


def three_parts(x):
    first = x.astype(BF16)
    rest = x - first.astype(F32)
    second = rest.astype(BF16)
    third = (rest - second.astype(F32)).astype(BF16)
    return jnp.concatenate([first, second, third], axis=0)


def part_widths(qhalf):
    if qhalf == 8 * LANES:
        return (4 * LANES, 4 * LANES)
    return (LANES,) * (qhalf // LANES)


def gather_plan(nt):
    if nt == 16:
        return {0: (8, 4, -4, 1, -1, 2, -2), -4: (1, -1, 2), 4: (1, -1, -2), 8: (1, -1)}
    return {0: tuple(sorted(range(1, nt), key=lambda k: -min(k, nt - k)))}


def kernel(
    nt, ne, cap, units, half,
    og_in, rt_in, gc_in, cs_in, hs, dw,
    hg_out, sg_out, gg_out,
    og, rt, gc, cs, W, S, HS, QZ, SL, TM, TOKP, SRCP, QT, PMSG, PX, XP, QS, XQ, ACC, GB, HG,
    SPART, SPX, SSUM, SRECV, GM, GV, PV, PVR, CH, NM,
    lsem, wsem, ssem, zsem, qasem, qbsem, pxsem, prsem, psend, xqsem,
    gxsem, gzsem, spsem, srsem,
):
    d = lax.axis_index("dp")
    e = lax.axis_index("expert")
    t = lax.axis_index("tensor")
    side = math.isqrt(ne)
    ex, ey = lax.div(e, side), lax.rem(e, side)
    group = 8 * nt
    slots = ne * cap
    n_chunks = nt // 2
    chunk_w = 2 * LANES
    per_half = n_chunks // 2
    phalf = per_half * chunk_w
    qhalf = half - phalf
    widths = part_widths(qhalf)
    offsets = [phalf + sum(widths[:i]) for i in range(len(widths))]
    last = len(widths) - 1
    blocks = half // LANES
    reach = n_chunks // 2
    other = 1 - d

    def zpeer(k):
        return lax.rem(t + k + nt, nt)

    def xpeer(o):
        return lax.rem(ex + o // side, side) * side + lax.rem(ey + o % side, side)

    def at_z(k):
        return (d, e, zpeer(k))

    def at_x(o):
        return (d, xpeer(o), t)

    partner = (other, e, t)
    right, left = at_z(1), at_z(-1)

    def arrived(ref, sems):
        remote(ref, ref, sems.at[0], sems.at[1], partner).wait_recv()

    def left_here(ref, sems):
        remote(ref, ref, sems.at[0], sems.at[1], partner).wait_send()

    barrier = pltpu.get_barrier_semaphore()
    for k in sorted(range(1, nt), key=lambda k: -min(k, nt - k)):
        pl.semaphore_signal(barrier, inc=1, device_id=at_z(k), device_id_type=MESH)
    for o in range(ne - 1, 0, -1):
        pl.semaphore_signal(barrier, inc=1, device_id=at_x(o), device_id_type=MESH)
    pl.semaphore_signal(barrier, inc=1, device_id=partner, device_id_type=MESH)

    pairs = ((og_in, og), (cs_in, cs), (rt_in, rt), (gc_in, gc), (dw, W.at[d]), (hs, HS))
    loads = [pltpu.make_async_copy(a, b, lsem.at[i]) for i, (a, b) in enumerate(pairs)]
    for load in loads:
        load.start()
    for load in loads[:4]:
        load.wait()

    def two_rows(first, second, width):
        upper = og[:, first : first + width].astype(F32)
        lower = og[:, second : second + width].astype(F32)
        return jnp.concatenate([upper, lower], axis=0).astype(BF16)

    for i, width in enumerate(widths):
        QT[i][t] = two_rows(offsets[i], half + offsets[i], width)
    for j in range(n_chunks):
        start = (j // per_half) * half + (j % per_half) * chunk_w
        SRCP[j] = two_rows(start, start + LANES, LANES)
    TOKP[t] = SRCP[lax.rem(t, n_chunks)]
    S[d] = jnp.broadcast_to(cs[...].astype(F32), (8, half))

    pl.semaphore_wait(barrier, nt + ne - 1)

    plan = gather_plan(nt)
    via = [rel for rel in plan if rel]

    def send_tokens(i, rel):
        chunk = QT[i].at[zpeer(rel)]
        for k in plan[rel]:
            seen = -k if k != 8 else 8
            known = rel == 0 and seen in via
            recv = qasem.at[i, via.index(seen)] if known else qbsem.at[i, 1]
            remote(chunk, chunk, qbsem.at[i, 0], recv, at_z(k)).start()

    def tokens_from(i, rels):
        for rel in rels:
            chunk = QT[i].at[zpeer(rel)]
            sem = qasem.at[i, via.index(rel)]
            remote(chunk, chunk, qbsem.at[i, 0], sem, partner).wait_recv()
            send_tokens(i, rel)

    for k in range(1, nt):
        source = SRCP.at[lax.rem(zpeer(k), n_chunks)]
        remote(source, TOKP.at[t], zsem.at[0], zsem.at[1], at_z(k)).start()
    for i in range(len(widths)):
        send_tokens(i, 0)
    remote(S.at[d], S.at[d], ssem.at[0], ssem.at[1], partner).start()
    remote(dw, W.at[d], wsem.at[0], wsem.at[1], partner).start()

    wide = 2 * group + group
    column = iota((group, wide), 1)
    token_of = jnp.where(
        column < 2 * group,
        lax.shift_right_logical(column, 4) * 8 + jnp.bitwise_and(column, 7),
        column - 2 * group,
    )
    row = iota((group, wide), 0)
    same = jnp.where(row == token_of, 1.0, 0.0).astype(BF16)
    earlier = jnp.where(row < token_of, 1.0, 0.0).astype(BF16)
    routes = jnp.dot(rt[...].astype(F32).astype(BF16), same, preferred_element_type=F32)
    codes = gc[...].astype(F32)
    name = [routes[k : k + 1] for k in (0, 1)]
    gate = [codes[k : k + 1] for k in (0, 1)]
    expert_row = iota((ne, wide), 0).astype(F32)
    names = [jnp.where(expert_row == name[k], 1.0, 0.0) for k in (0, 1)]
    both = (names[0] + names[1])[:, 2 * group :].astype(BF16)
    before = jnp.dot(both, earlier, preferred_element_type=F32)
    place = [jnp.sum(names[k] * before, axis=0, keepdims=True) for k in (0, 1)]
    slot = [name[k] * float(cap) + place[k] for k in (0, 1)]
    slot_row = iota((slots, wide), 0).astype(F32)
    picks = [jnp.where(slot_row == slot[k], 1.0, 0.0) for k in (0, 1)]
    pick = picks[0] + picks[1]
    in_half = jnp.bitwise_and(lax.shift_right_logical(iota((slots, 2 * group), 1), 3), 1)
    pick_q = [jnp.where(in_half == a, pick[:, : 2 * group], 0.0).astype(BF16) for a in (0, 1)]
    gate_pick = (
        picks[0][:, 2 * group :] * gate[0] + picks[1][:, 2 * group :] * gate[1]
    ).astype(BF16)
    gates = jnp.dot(gate_pick, jnp.ones((group, LANES), BF16), preferred_element_type=F32)
    PMSG[:, 2 * cap :, :] = (gates * (1.0 / 256.0)).astype(BF16).reshape(ne, cap, LANES)

    place_row = iota((LANES, group), 0).astype(F32)
    for k in (0, 1):
        at = slice(k * group, (k + 1) * group)
        CH[:, at] = jnp.where(place_row == place[k][:, 2 * group :], 1.0, 0.0).astype(BF16)
        NM[:, at] = names[k][:, 2 * group :]
    for load in loads[4:]:
        load.wait()

    def unit(hh, block):
        lanes = slice(block * 256, block * 256 + 256)
        scale = S[hh, 0:1, lanes]
        inverse = 1.0 / scale

        def rows(i, carry):
            at = pl.ds(pl.multiple_of(i * 128, 128), 128)
            u = W[hh, at, lanes].astype(F32) * inverse
            b = jnp.tanh(u)
            QZ[hh, at, lanes] = (scale * b).astype(BF16)
            SL[at, :] = (b - u * (1.0 - b * b)).astype(BF16)
            return carry

        lax.fori_loop(0, units // 128, rows, 0, unroll=True)
        TM[hh, :, lanes] = jnp.dot(HS[...], SL[...], preferred_element_type=F32)

    def partner_ready():
        arrived(S.at[other], ssem)
        arrived(W.at[other], wsem)

    def terms(x, hh, start):
        scaled = (x.astype(F32) * GB[...]).astype(BF16).astype(F32)
        return jnp.sum(scaled * TM[hh, :, pl.ds(start, LANES)], axis=0, keepdims=True)

    def chunk_p(j):
        hh = lax.div(j, per_half)
        b = lax.rem(j, per_half)
        start = pl.multiple_of(b * chunk_w, chunk_w)
        for i in (0, 1):
            x = XP[j, :, i * LANES : (i + 1) * LANES]
            SPART[hh, 2 * b + i] = terms(x, hh, pl.multiple_of(start + i * LANES, LANES))
        ACC[...] += lax.dot_general(
            XP[j],
            QZ[hh, :, pl.ds(start, chunk_w)],
            (((1,), (1,)), ((), ())),
            preferred_element_type=F32,
        )

    def parts_q(i):
        width = widths[i]
        for a in (0, 1):
            for c in range(width // LANES):
                at = offsets[i] + c * LANES
                x = XQ[i][:, :, a * width + c * LANES : a * width + (c + 1) * LANES]
                SPART[a, at // LANES] = terms(x.reshape(slots, LANES), a, at)

    cuts = 1

    def dot_q(i, cut):
        lanes = slice(offsets[i], offsets[i] + widths[i])
        at = slice(cut * units // cuts, (cut + 1) * units // cuts)
        ACC[:, at] += lax.dot_general(
            XQ[i][...].reshape(slots, 2 * widths[i]),
            jnp.concatenate([QZ[0, at, lanes], QZ[1, at, lanes]], axis=1),
            (((1,), (1,)), ((), ())),
            preferred_element_type=F32,
        )

    def arrived_q(i):
        arrived(XQ[i].at[pl.ds(0, ne - 1)], xqsem.at[i])

    pb, qb = phalf // 256, qhalf // 256
    work = [functools.partial(unit, d, b) for b in range(pb)]
    work += [partner_ready]
    work += [functools.partial(unit, other, b) for b in range(pb)]
    work += [functools.partial(unit, h, pb + b) for b in range(qb) for h in (d, other)]
    chunks = [functools.partial(chunk_p, lax.rem(t, n_chunks))]
    for k in range(1, reach):
        for rel in (-k, k):
            chunks += [functools.partial(chunk_p, lax.rem(zpeer(rel), n_chunks))]
    chunks += [functools.partial(chunk_p, lax.rem(zpeer(reach), n_chunks))]

    def do(jobs, n):
        for _ in range(n):
            if jobs:
                jobs.pop(0)()


    do(work, pb)

    tokens_from(0, via[:2])

    arrived(TOKP.at[pl.ds(0, nt - 1)], zsem)
    tokens = TOKP[...].reshape(2 * group, LANES)
    for a in (0, 1):
        routed = jnp.dot(pick_q[a], tokens, preferred_element_type=F32).astype(BF16)
        PMSG[:, a * cap : (a + 1) * cap, :] = routed.reshape(ne, cap, LANES)
    for o in range(1, ne):
        remote(PMSG.at[xpeer(o)], PX.at[e], pxsem.at[0], pxsem.at[1], at_x(o)).start()
    PX[e] = PMSG[e]

    def route_q(i):
        width = widths[i]
        arrived(QT[i].at[pl.ds(0, nt - 1 - len(via))], qbsem.at[i])
        gathered = QT[i][...].reshape(2 * group, width)
        for a in (0, 1):
            QS[i][:, :, a * width : (a + 1) * width] = (
                jnp.dot(pick_q[a], gathered, preferred_element_type=F32)
                .astype(BF16)
                .reshape(ne, cap, width)
            )
        for o in range(1, ne):
            source, target = QS[i].at[xpeer(o)], XQ[i].at[e]
            remote(source, target, xqsem.at[i, 0], xqsem.at[i, 1], at_x(o)).start()
        XQ[i][e] = QS[i][e]

    tokens_from(0, via[2:])
    for i in range(1, len(widths)):
        tokens_from(i, via)
    do(work, 1 + pb)

    pieces = 8
    prow = slots // pieces

    def piece(j, i):
        return XP.at[j, pl.ds(i * prow, prow)]

    def pass_on(way, rel, k, i):
        if k == reach and (i < pieces // 2) != (way == 0):
            return
        ref = piece(lax.rem(zpeer(rel), n_chunks), i)
        remote(ref, ref, psend.at[way], prsem.at[way, k, i], (right, left)[way]).start()

    def ring_p(k, jobs):
        jobs = list(jobs)
        for i in range(pieces):
            for way in (0, 1):
                if k == reach and (i < pieces // 2) != (way == 0):
                    continue
                rel = -k if way == 0 else k
                ref = piece(lax.rem(zpeer(rel), n_chunks), i)
                remote(ref, ref, psend.at[way], prsem.at[way, k, i], partner).wait_recv()
                if k < reach:
                    pass_on(way, rel, k + 1, i)
            do(jobs, 1)
        do(jobs, len(jobs))

    arrived(PX.at[pl.ds(0, ne - 1)], pxsem)
    mine_p = lax.rem(t, n_chunks)
    for a in (0, 1):
        XP[mine_p, :, a * LANES : (a + 1) * LANES] = PX[:, a * cap : (a + 1) * cap, :].reshape(slots, LANES)
    for i in range(pieces):
        for way in (0, 1):
            pass_on(way, 0, 1, i)
    route_q(0)
    GB[...] = PX[:, 2 * cap :, :].reshape(slots, LANES).astype(F32)
    ACC[...] = jnp.zeros_like(ACC)
    for i in range(1, len(widths)):
        route_q(i)

    def idle():
        pass

    def jobs_q(i):
        jobs = [functools.partial(arrived_q, i), functools.partial(parts_q, i)]
        return jobs + [functools.partial(dot_q, i, cut) for cut in range(cuts)]

    pending = [jobs_q(i) for i in range(last)]
    for k in range(1, reach + 1):
        jobs = work + [chunks[0]]
        if k > 1:
            jobs = [chunks[2 * k - 3], idle, chunks[2 * k - 2], idle]
        if k == reach - 1:
            jobs = jobs + pending.pop(0)
        ring_p(k, jobs)
    for jobs in pending:
        do(jobs, len(jobs))
    do([chunks[-1]], 1)
    arrived_q(last)
    for cut in range(cuts):
        dot_q(last, cut)

    weighed = ACC[:, 0:LANES] * HS[:, 0:LANES].astype(F32)
    for c in range(LANES, units, LANES):
        weighed += ACC[:, c : c + LANES] * HS[:, c : c + LANES].astype(F32)
    weighed = jnp.sum(weighed, axis=1, keepdims=True)
    at_place = jnp.bitwise_and(iota((slots, LANES), 0), cap - 1) == iota((slots, LANES), 1)
    GM[...] = jnp.sum(
        jnp.where(at_place, weighed, 0.0).reshape(ne, cap, LANES), axis=1, keepdims=True
    )
    for o in range(1, ne):
        remote(GM.at[xpeer(o)], GV.at[e], gxsem.at[0], gxsem.at[1], at_x(o)).start()
    GV[e] = GM[e]

    parts_q(last)
    remote(SPART.at[other], SPX, spsem.at[0], spsem.at[1], partner).start()
    arrived(SPX, spsem)
    SSUM[...] = SPART[d] + SPX[...]
    for k in range(1, nt):
        remote(SSUM, SRECV.at[t], srsem.at[0], srsem.at[1], at_z(k)).start()
    SRECV[t] = SSUM[...]

    for c in range(0, units, LANES):
        HG[:, c : c + LANES] = (ACC[:, c : c + LANES] * GB[...]).astype(BF16)
    save = pltpu.make_async_copy(HG, hg_out, lsem.at[0])
    save.start()

    left_here(TOKP.at[pl.ds(0, nt - 1)], zsem)
    left_here(S.at[d], ssem)
    left_here(dw, wsem)
    left_here(PMSG.at[pl.ds(0, ne - 1)], pxsem)
    for i in range(len(widths)):
        left_here(QT[i].at[pl.ds(0, nt - 1)], qbsem.at[i])
        left_here(QS[i].at[pl.ds(0, ne - 1)], xqsem.at[i])
    for way in (0, 1):
        ref = XP.at[pl.ds(0, 2 * reach - 1), pl.ds(0, slots // 2)]
        remote(ref, ref, psend.at[way], prsem.at[way, 1, 0], partner).wait_send()

    arrived(GV.at[pl.ds(0, ne - 1)], gxsem)
    values = jnp.concatenate([GV[i] for i in range(ne)], axis=0)
    spread = jnp.dot(three_parts(values), CH[...], preferred_element_type=F32)
    spread = (spread[:ne] + spread[ne : 2 * ne] + spread[2 * ne :]) * NM[...]
    pair_row = jnp.sum(spread, axis=0, keepdims=True)
    pair_rows = [pair_row[:, :group], pair_row[:, group:]]
    PV[...] = jnp.concatenate(pair_rows, axis=0)
    for k in range(1, nt):
        remote(PV, PVR.at[t], gzsem.at[0], gzsem.at[1], at_z(k)).start()
    PVR[t] = PV[...]

    arrived(SRECV.at[pl.ds(0, nt - 1)], srsem)
    total = SRECV[0]
    for i in range(1, nt):
        total += SRECV[i]
    for i in range(blocks):
        sg_out[:, i * LANES : (i + 1) * LANES] = total[i]

    arrived(PVR.at[pl.ds(0, nt - 1)], gzsem)
    total = PVR[0]
    for i in range(1, nt):
        total += PVR[i]
    mine = jnp.where(iota((group, 8), 0) == t * 8 + iota((group, 8), 1), 1.0, 0.0).astype(BF16)
    picked = jnp.dot(three_parts(total), mine, preferred_element_type=F32)
    gg_out[...] = picked[0:2] + picked[2:4] + picked[4:6]

    left_here(GM.at[pl.ds(0, ne - 1)], gxsem)
    left_here(PVR.at[pl.ds(0, nt - 1)], gzsem)
    left_here(SPX, spsem)
    left_here(SRECV.at[pl.ds(0, nt - 1)], srsem)
    save.wait()


def write_kernel(hg, sg, gg, hg_out, sg_out, gg_out):
    hg_out[...] = hg[...]
    sg_out[...] = sg[...]
    gg_out[...] = gg[...]


def on_device(nt, ne, out_grad, routing, gate_codes, hidden_saved, down_weight, channel_scale):
    cap = hidden_saved.shape[3]
    units = hidden_saved.shape[4]
    half = down_weight.shape[2]
    group = routing.shape[0]
    slots = ne * cap
    n_chunks = nt // 2
    widths = part_widths(half - n_chunks * LANES)
    blocks = half // LANES
    vmem = pl.BlockSpec(memory_space=pltpu.VMEM)
    anywhere = pl.BlockSpec(memory_space=pl.ANY)
    dma = pltpu.SemaphoreType.DMA
    results = (
        jax.ShapeDtypeStruct((slots, units), BF16),
        jax.ShapeDtypeStruct((1, half), F32),
        jax.ShapeDtypeStruct((2, 8), F32),
    )
    parts = pl.pallas_call(
        functools.partial(kernel, nt, ne, cap, units, half),
        out_shape=results,
        in_specs=[anywhere] * 6,
        out_specs=(anywhere, vmem, vmem),
        scratch_shapes=[
            pltpu.VMEM(out_grad.shape, BF16),
            pltpu.VMEM((2, group), jnp.int32),
            pltpu.VMEM((2, group), jnp.int32),
            pltpu.VMEM((1, half), BF16),
            pltpu.VMEM((2, units, half), BF16),
            pltpu.VMEM((2, 8, half), F32),
            pltpu.VMEM((slots, units), BF16),
            pltpu.VMEM((2, units, half), BF16),
            pltpu.VMEM((units, 256), BF16),
            pltpu.VMEM((2, slots, half), F32),
            pltpu.VMEM((nt, 16, LANES), BF16),
            pltpu.VMEM((n_chunks, 16, LANES), BF16),
            [pltpu.VMEM((nt, 16, w), BF16) for w in widths],
            pltpu.VMEM((ne, 3 * cap, LANES), BF16),
            pltpu.VMEM((ne, 3 * cap, LANES), BF16),
            pltpu.VMEM((n_chunks, slots, 2 * LANES), BF16),
            [pltpu.VMEM((ne, cap, 2 * w), BF16) for w in widths],
            [pltpu.VMEM((ne, cap, 2 * w), BF16) for w in widths],
            pltpu.VMEM((slots, units), F32),
            pltpu.VMEM((slots, LANES), F32),
            pltpu.VMEM((slots, units), BF16),
            pltpu.VMEM((2, blocks, 1, LANES), F32),
            pltpu.VMEM((blocks, 1, LANES), F32),
            pltpu.VMEM((blocks, 1, LANES), F32),
            pltpu.VMEM((nt, blocks, 1, LANES), F32),
            pltpu.VMEM((ne, 1, LANES), F32),
            pltpu.VMEM((ne, 1, LANES), F32),
            pltpu.VMEM((2, group), F32),
            pltpu.VMEM((nt, 2, group), F32),
            pltpu.VMEM((LANES, 2 * group), BF16),
            pltpu.VMEM((ne, 2 * group), F32),
            dma((6,)),
            dma((2,)),
            dma((2,)),
            dma((2,)),
            dma((len(widths), 3)),
            dma((len(widths), 2)),
            dma((2,)),
            dma((2, n_chunks // 2 + 1, 8)),
            dma((2,)),
            dma((len(widths), 2)),
            dma((2,)),
            dma((2,)),
            dma((2,)),
            dma((2,)),
        ],
        compiler_params=pltpu.CompilerParams(
            collective_id=0, has_side_effects=True, vmem_limit_bytes=60 * 1024 * 1024
        ),
    )(
        out_grad,
        routing.T,
        gate_codes.T,
        channel_scale,
        hidden_saved.reshape(slots, units),
        down_weight.reshape(units, half),
    )
    hidden_grad, scale_grad, gate_grad = pl.pallas_call(
        write_kernel,
        out_shape=results,
        in_specs=[vmem] * 3,
        out_specs=(vmem,) * 3,
    )(*parts)
    return hidden_grad.reshape(hidden_saved.shape), scale_grad, gate_grad.T


def solution(mesh):
    in_specs = (
        P(("dp", "expert", "tensor"), None),
        P(("dp", "expert"), None),
        P(("dp", "expert"), None),
        P("dp", "expert", None, None, "tensor"),
        P("expert", "tensor", "dp"),
        P("expert", "dp"),
    )
    out_specs = (
        P("dp", "expert", None, None, "tensor"),
        P("expert", "dp"),
        P(("dp", "expert", "tensor"), None),
    )
    return jax.shard_map(
        functools.partial(on_device, mesh.shape["tensor"], mesh.shape["expert"]),
        mesh=mesh,
        in_specs=in_specs,
        out_specs=out_specs,
        check_vma=False,
    )
```
